32 devices in a mesh: tm: 4 (over x, core), space: 8 (over z, y).
Axes of the slice: x: 2, y: 2, z: 4, core: 2. Of those that a mesh axis runs over, the one named last changes fastest.
Arguments:
- water_depth: float32 [24, 16, 128], P('space'), may hold values from 0.7 to 1.4
- momentum: float32 [24, 2, 16, 128], P('space'), may hold values from -0.6 to 0.6
- slot_live: int32 [24], P('space'), may hold values from 0 to 1, as said below
- neighbours: int32 [24, 2], P('space'), may hold values from 0 to 3, as said below
Outputs:
- slice_ends: float32 [4, 24, 3, 16, 128], P('tm', 'space')
The draws below stay inside these ranges and needn't reach their ends.
Inputs may be any that keep to these rules, and one draw needn't show every extreme that they name: `slot_live`: every owner's 3 consecutive slots hold between 1 and 3 live blocks; owners 2p and 2p + 1 together hold exactly 4 live blocks, and some owner holds 3. `neighbours`: the live blocks of each owner form one run along the channel, and the runs of owners 0, 1, 2 and so on follow one another around the periodic channel. For a live slot, entry 0 names the slot of the same owner holding the block to the west and entry 1 the one to the east, or 3 where that block belongs to the previous (west) or next (east) owner; each owner has exactly one live slot with entry 0 equal to 3 and one with entry 1 equal to 3. A dead slot names itself in both entries.
All inputs are finite; a program needn't handle non-finite values.
Results may differ from the reference program's by a relative error of at most 0.00002.
Values sent between devices are 32-bit elements; how exact they have to be, the bound alone decides.
No kernel may reach another device: no remote copies, remote signals or barrier semaphores. Data moves between devices by JAX's collectives and lax.ppermute only.
A program may use at most 64 MiB of HBM per device.

```python
import jax
import jax.numpy as jnp
from jax import lax

BS = 128
BY = 16
SUB = 3
KITER = 2
BLK_DEV = 3
SLOTS = 24
N_TM = 4


def block_layout(key):
    owners = SLOTS // BLK_DEV
    pair_count = owners // 2
    balanced = (BLK_DEV + 1) // 2
    leading = jax.random.randint(jax.random.fold_in(key, 101), (pair_count,), 1, 2 * balanced)
    fullest = jax.random.randint(jax.random.fold_in(key, 102), (), 0, pair_count)
    leading = jnp.where(jnp.arange(pair_count) == fullest, 2 * balanced - 1, leading)
    swapped = jax.random.randint(jax.random.fold_in(key, 103), (pair_count,), 0, 2)
    first_count = jnp.where(swapped == 1, 2 * balanced - leading, leading)
    live_count = jnp.stack([first_count, 2 * balanced - first_count], axis=1).reshape(owners)
    scores = jax.random.randint(jax.random.fold_in(key, 104), (owners, BLK_DEV), 0, 65536)
    run_order = jnp.argsort(scores * BLK_DEV + jnp.arange(BLK_DEV)[None, :], axis=1).astype(jnp.int32)
    position = jnp.argsort(run_order, axis=1).astype(jnp.int32)
    live_slot = position < live_count[:, None]
    own_slot = jnp.broadcast_to(jnp.arange(BLK_DEV, dtype=jnp.int32)[None, :], (owners, BLK_DEV))
    preceding = jnp.take_along_axis(run_order, jnp.maximum(position - 1, 0), axis=1)
    following = jnp.take_along_axis(run_order, jnp.minimum(position + 1, BLK_DEV - 1), axis=1)
    west_slot = jnp.where(position > 0, preceding, BLK_DEV)
    east_slot = jnp.where(position < live_count[:, None] - 1, following, BLK_DEV)
    west_slot = jnp.where(live_slot, west_slot, own_slot).astype(jnp.int32)
    east_slot = jnp.where(live_slot, east_slot, own_slot).astype(jnp.int32)
    return (live_slot.astype(jnp.int32).reshape(SLOTS), jnp.stack([west_slot, east_slot], axis=-1).reshape(SLOTS, 2))


def draw_slot_live(key, part):
    return block_layout(key)[0]


def draw_neighbours(key, part):
    return block_layout(key)[1]


def draw_water_depth(key, part):
    rough = jax.random.uniform(jax.random.fold_in(key, 201), (SLOTS, BY, BS), jnp.float32)
    return (0.7 + 0.7 * rough).astype(jnp.float32)


def shard_levels(stream_key, extent, cuts, low, top_value):
    gain, own = 1.0, jax.random.fold_in(stream_key, 6)
    for dim, shards_of in cuts:
        steps = jnp.exp(jax.random.uniform(jax.random.fold_in(own, dim), (shards_of,), jnp.float32, low / len(cuts), top_value / len(cuts)))
        gain = gain * jnp.repeat(steps, extent[dim] // shards_of).reshape([-1 if axis == dim else 1 for axis in range(len(extent))])
    return gain


def centred(stream_key, shape, spread, reach, cuts=(), kind=jnp.bfloat16):
    result = spread * jax.random.normal(stream_key, shape, jnp.float32)
    if cuts:
        result = result * shard_levels(stream_key, shape, cuts, -0.22, 0.18)
    return jnp.clip(result, -reach, reach).astype(kind)


def setup_inputs(seed: int = 0) -> dict:
    key_list = jax.random.split(jax.random.key(seed), 5)
    return {
        "water_depth": draw_water_depth(jax.random.fold_in(key_list[4], 71), 0),
        "momentum": centred(key_list[1], (SLOTS, 2, BY, BS), 0.15, 0.6, ((0, 8),), jnp.float32),
        "slot_live": draw_slot_live(jax.random.fold_in(key_list[4], 71), 0),
        "neighbours": draw_neighbours(jax.random.fold_in(key_list[4], 71), 0),
    }


GRAVITY = 1.0
TIME_STEP = 0.15

def fluxes(fields, along_ratio, across_ratio):
    height = fields[0]
    drift_along = fields[1] / height
    drift_across = fields[2] / height
    celerity = jnp.sqrt(GRAVITY * height)
    pressure = 0.5 * GRAVITY * height * height
    flux_along = jnp.stack([fields[1], fields[1] * drift_along + pressure, fields[2] * drift_along])
    signal_along = jnp.abs(drift_along) + celerity
    face_along = 0.5 * (flux_along[:, :, :-1] + flux_along[:, :, 1:]) - 0.5 * jnp.maximum(signal_along[:, :-1], signal_along[:, 1:]) * (fields[:, :, 1:] - fields[:, :, :-1])
    interior = fields[:, :, 1:-1]
    flux_across = jnp.stack([fields[2], fields[1] * drift_across, fields[2] * drift_across + pressure])[:, :, 1:-1]
    signal_across = (jnp.abs(drift_across) + celerity)[:, 1:-1]
    mirror = jnp.array([1.0, 1.0, -1.0], dtype=jnp.float32)[:, None, None]
    padded = jnp.concatenate([interior[:, :1] * mirror, interior, interior[:, -1:] * mirror], axis=1)
    padded_flux = jnp.concatenate([-flux_across[:, :1] * mirror, flux_across, -flux_across[:, -1:] * mirror], axis=1)
    padded_signal = jnp.concatenate([signal_across[:1], signal_across, signal_across[-1:]], axis=0)
    face_across = 0.5 * (padded_flux[:, :-1] + padded_flux[:, 1:]) - 0.5 * jnp.maximum(padded_signal[:-1], padded_signal[1:]) * (padded[:, 1:] - padded[:, :-1])
    return -along_ratio * (face_along[:, :, 1:] - face_along[:, :, :-1]) - across_ratio * (face_across[:, 1:] - face_across[:, :-1])

def heun_step(fields, along_ratio, across_ratio):
    predictor = fields[:, :, 1:-1] + fluxes(fields, along_ratio, across_ratio)
    return 0.5 * (fields[:, :, 2:-2] + predictor[:, :, 1:-1] + fluxes(predictor, along_ratio, across_ratio))

def fine_block(fields):
    for substep in range(SUB):
        fields = heun_step(fields, TIME_STEP, TIME_STEP)
    return fields

def coarse_block(fields):
    return heun_step(fields, TIME_STEP * SUB, TIME_STEP * SUB / 3.0)

def restrict(fields):
    return 0.5 * (fields[..., 0::2, :] + fields[..., 1::2, :])

def prolong(fields):
    return jnp.repeat(fields, 2, axis=-2)

def links(slot_live, neighbours):
    total = slot_live.shape[0]
    owners = total // BLK_DEV
    slot_ids = jnp.arange(total, dtype=jnp.int32)
    owner_id = slot_ids // BLK_DEV
    live_slot = slot_live == 1
    first_block = jnp.logical_and(neighbours[:, 0] == BLK_DEV, live_slot)
    last_block = jnp.logical_and(neighbours[:, 1] == BLK_DEV, live_slot)
    first_index = lax.optimization_barrier(jnp.sum(jnp.where(first_block, slot_ids, 0).reshape(owners, BLK_DEV), axis=1)).astype(jnp.int32)
    last_index = lax.optimization_barrier(jnp.sum(jnp.where(last_block, slot_ids, 0).reshape(owners, BLK_DEV), axis=1)).astype(jnp.int32)
    prior_owner = (owner_id + owners - 1) % owners
    next_owner = (owner_id + 1) % owners
    west_slot = jnp.where(neighbours[:, 0] < BLK_DEV, owner_id * BLK_DEV + neighbours[:, 0], last_index[prior_owner])
    east_slot = jnp.where(neighbours[:, 1] < BLK_DEV, owner_id * BLK_DEV + neighbours[:, 1], first_index[next_owner])
    return (west_slot.astype(jnp.int32), east_slot.astype(jnp.int32))

def extend(fields, west_slot, east_slot, rim_width):
    west_rim = jnp.take(fields[..., -rim_width:], west_slot, axis=0)
    east_rim = jnp.take(fields[..., :rim_width], east_slot, axis=0)
    return jnp.concatenate([west_rim, fields, east_rim], axis=-1)

def reference(water_depth, momentum, slot_live, neighbours):
    initial = jnp.concatenate([water_depth[:, None], momentum], axis=1)
    west_slot, east_slot = links(slot_live, neighbours)

    def coarse_all(fields):
        return jax.vmap(coarse_block)(extend(fields, west_slot, east_slot, 2))

    def fine_all(fields):
        return lax.map(fine_block, extend(fields, west_slot, east_slot, 2 * SUB))
    coarse_start = restrict(initial)
    previous = []
    slice_start = [initial]
    current = coarse_start
    for position in range(N_TM):
        propagated = coarse_all(current)
        previous.append(propagated)
        current = propagated
        if position + 1 < N_TM:
            slice_start.append(prolong(current))
    slice_end = []
    for sweep in range(KITER):
        refined = [fine_all(slice_start[position]) for position in range(N_TM)]
        renewed = []
        current = coarse_start
        for position in range(N_TM):
            propagated = coarse_all(current)
            renewed.append(propagated)
            current = propagated + (restrict(refined[position]) - previous[position])
        slice_end = [prolong(renewed[position]) + refined[position] - prolong(previous[position]) for position in range(N_TM)]
        slice_start = [initial] + slice_end[:-1]
        previous = renewed
    live_mask = (slot_live == 1)[:, None, None, None]
    return jnp.stack([jnp.where(live_mask, ending, 0.0) for ending in slice_end])
```

```python
import functools

import jax
import jax.numpy as jnp
from jax import lax
from jax.experimental import pallas as pl
from jax.experimental.pallas import tpu as pltpu
from jax.sharding import PartitionSpec as P

SUB = 3
KITER = 2
TIME_STEP = 0.15


def lane_of(shape):
    return lax.broadcasted_iota(jnp.int32, shape, 1)


def row_of(shape):
    return lax.broadcasted_iota(jnp.int32, shape, 0)


class Scheme:
    def __init__(self, shape, linked):
        self.rows, self.lanes = shape
        self.linked = linked
        lane, row = lane_of(shape), row_of(shape)
        self.is_first_lane = lane == 0
        self.is_last_lane = lane == self.lanes - 1
        self.is_first_row = row == 0
        self.is_last_row = row == self.rows - 1

    def east(self, tiles):
        rolled = [pltpu.roll(tile, self.lanes - 1, 1) for tile in tiles]
        if not self.linked:
            return rolled
        return [
            jnp.where(self.is_last_lane, rolled[k + 1], rolled[k]) if k + 1 < len(rolled) else rolled[k]
            for k in range(len(rolled))
        ]

    def west(self, tiles):
        rolled = [pltpu.roll(tile, 1, 1) for tile in tiles]
        if not self.linked:
            return rolled
        return [jnp.where(self.is_first_lane, rolled[k - 1], rolled[k]) if k else rolled[k] for k in range(len(rolled))]

    def above(self, tile):
        return pltpu.roll(tile, self.rows - 1, 0)

    def below(self, tile):
        return pltpu.roll(tile, 1, 0)

    def derived(self, state):
        out = []
        for h, hu, hv in zip(*state):
            root = lax.rsqrt(h)
            celerity = h * root
            inverse = root * root
            u = hu * inverse
            q = hv * inverse
            p = (0.5 * h) * h
            out.append(
                (h, hu, hv, hu * u + p, hv * u, hv * q + p, jnp.abs(u) + celerity, jnp.abs(q) + celerity)
            )
        return out

    def along(self, parts):
        h, hu, hv, f1, f2, _, speed, _ = ([part[i] for part in parts] for i in range(8))
        speed_e = self.east(speed)
        values_e = [self.east(h), self.east(hu), self.east(hv)]
        fluxes_e = [values_e[1], self.east(f1), self.east(f2)]
        bound = [jnp.maximum(a, b) for a, b in zip(speed, speed_e)]
        differences = []
        for value, flux, value_e, flux_e in zip((h, hu, hv), (hu, f1, f2), values_e, fluxes_e):
            face = [
                (f + fe) - m * (ve - v) for f, fe, m, v, ve in zip(flux, flux_e, bound, value, value_e)
            ]
            differences.append([e - w for e, w in zip(face, self.west(face))])
        return differences

    @staticmethod
    def cross(lower, upper):
        bound = jnp.maximum(lower[7], upper[7])
        return [
            (lower[f] + upper[f]) - bound * (upper[v] - lower[v]) for v, f in ((0, 2), (1, 4), (2, 5))
        ]

    def upper_faces(self, top, raised):
        faces = self.cross(top, raised)
        wall = 2.0 * (top[5] + top[7] * top[2])
        return [
            jnp.where(self.is_last_row, 0.0, faces[0]),
            jnp.where(self.is_last_row, 0.0, faces[1]),
            jnp.where(self.is_last_row, wall, faces[2]),
        ]

    def lower_faces(self, bottom, faces):
        wall = 2.0 * (bottom[5] - bottom[7] * bottom[2])
        lowered = [self.below(face) for face in faces]
        return [lowered[0], lowered[1], jnp.where(self.is_first_row, wall, lowered[2])]

    def raise_up(self, part):
        return [self.above(part[i]) if i in (0, 1, 2, 4, 5, 7) else None for i in range(8)]

    def fine_rhs(self, even, odd):
        even_parts, odd_parts = self.derived(even), self.derived(odd)
        even_x, odd_x = self.along(even_parts), self.along(odd_parts)
        even_out, odd_out = [[], [], []], [[], [], []]
        scale = -0.5 * TIME_STEP
        for k, (a, b) in enumerate(zip(even_parts, odd_parts)):
            inner = self.cross(a, b)
            upper = self.upper_faces(b, self.raise_up(a))
            lower = self.lower_faces(a, upper)
            for i in range(3):
                even_out[i].append(scale * (even_x[i][k] + (inner[i] - lower[i])))
                odd_out[i].append(scale * (odd_x[i][k] + (upper[i] - inner[i])))
        return even_out, odd_out

    def coarse_rhs(self, state):
        parts = self.derived(state)
        x = self.along(parts)
        out = [[], [], []]
        scale_x, scale_y = -0.5 * TIME_STEP * SUB, -0.5 * TIME_STEP * SUB / 3.0
        for k, a in enumerate(parts):
            upper = self.upper_faces(a, self.raise_up(a))
            lower = self.lower_faces(a, upper)
            for i in range(3):
                out[i].append(scale_x * x[i][k] + scale_y * (upper[i] - lower[i]))
        return out

    @staticmethod
    def plus(a, b):
        return [[s + t for s, t in zip(u, v)] for u, v in zip(a, b)]

    @staticmethod
    def minus(a, b):
        return [[s - t for s, t in zip(u, v)] for u, v in zip(a, b)]

    @staticmethod
    def half(a):
        return [[0.5 * s for s in u] for u in a]

    def coarse(self, state):
        first = self.plus(state, self.coarse_rhs(state))
        return self.half(self.plus(self.plus(state, first), self.coarse_rhs(first)))

    def fine(self, pair):
        for _ in range(SUB):
            first = [self.plus(s, r) for s, r in zip(pair, self.fine_rhs(*pair))]
            pair = [
                self.half(self.plus(self.plus(s, f), r)) for s, f, r in zip(pair, first, self.fine_rhs(*first))
            ]
        return pair

    def restrict(self, pair):
        return self.half(self.plus(pair[0], pair[1]))


class Parareal:
    def __init__(self, scheme, initial):
        self.scheme = scheme
        self.initial = initial
        self.known = {}

    def memo(self, key, build):
        if key not in self.known:
            self.known[key] = build()
        return self.known[key]

    def coarse_state(self, sweep, n):
        sweep = min(sweep, n)

        def build():
            s = self.scheme
            if n == 0:
                return s.restrict(self.initial)
            stepped = self.coarse_step(sweep, n - 1)
            if sweep == 0:
                return stepped
            correction = s.minus(s.restrict(self.fine_run(sweep, n - 1)), self.coarse_step(sweep - 1, n - 1))
            return s.plus(stepped, correction)

        return self.memo(("c", sweep, n), build)

    def coarse_step(self, sweep, n):
        sweep = min(sweep, n)
        return self.memo(("k", sweep, n), lambda: self.scheme.coarse(self.coarse_state(sweep, n)))

    def fine_run(self, sweep, n):
        sweep = 1 if n == 0 else sweep

        def build():
            if n == 0:
                start = self.initial
            elif sweep == 1:
                state = self.coarse_state(0, n)
                start = [state, state]
            else:
                start = self.end(sweep - 1, n - 1)
            return self.scheme.fine(start)

        return self.memo(("f", sweep, n), build)

    def end(self, sweep, n):
        def build():
            s = self.scheme
            refined = self.fine_run(sweep, n)
            renewed, previous = self.coarse_step(sweep, n), self.coarse_step(sweep - 1, n)
            return [s.minus(s.plus(renewed, part), previous) for part in refined]

        return self.memo(("e", sweep, n), build)


def run_of(live_ref, near_ref, blocks):
    first = jnp.int32(0)
    last = jnp.int32(0)
    for slot in range(blocks):
        first = jnp.where((live_ref[slot] == 1) & (near_ref[slot, 0] == blocks), slot, first)
        last = jnp.where((live_ref[slot] == 1) & (near_ref[slot, 1] == blocks), slot, last)
    return first, last


def load_pair(depth_ref, momentum_ref, slot):
    rows = depth_ref.shape[1] // 2
    return [
        [
            depth_ref[slot, pl.ds(parity, rows, stride=2), :],
            momentum_ref[slot, 0, pl.ds(parity, rows, stride=2), :],
            momentum_ref[slot, 1, pl.ds(parity, rows, stride=2), :],
        ]
        for parity in range(2)
    ]


def pack(pieces, start, rim):
    rows, lanes = pieces[0].shape
    lane = lane_of((rows, lanes))
    per_tile = lanes // rim
    tiles = []
    for i, piece in enumerate(pieces):
        place = (i % per_tile) * rim
        moved = pltpu.roll(piece, (place - start) % lanes, 1)
        if place == 0:
            tiles.append(moved)
        else:
            tiles[-1] = jnp.where(lane >= place, moved, tiles[-1])
    return tiles


def unpack(packed_ref, index, place, rim):
    rows, lanes = packed_ref.shape[1:]
    per_tile = lanes // rim
    source = (index % per_tile) * rim
    return pltpu.roll(packed_ref[index // per_tile], (place - source) % lanes, 1)


def send_east_kernel(rim, depth_ref, momentum_ref, live_ref, near_ref, out_ref):
    blocks, _, lanes = depth_ref.shape
    _, last = run_of(live_ref, near_ref, blocks)
    even, odd = load_pair(depth_ref, momentum_ref, last)
    for i, tile in enumerate(pack([*even, *odd], lanes - rim, rim)):
        out_ref[i] = tile


def interior_kernel(
    rim, slices, depth_ref, momentum_ref, live_ref, near_ref, out_ref, send_ref, edge_ref
):
    blocks, height, lanes = depth_ref.shape
    rows = height // 2
    first, last = run_of(live_ref, near_ref, blocks)
    slots = [first]
    for _ in range(blocks - 1):
        following = near_ref[slots[-1], 1]
        slots.append(jnp.where(following < blocks, following, slots[-1]))
    count = sum(live_ref[slot] for slot in range(blocks))

    first_even, first_odd = load_pair(depth_ref, momentum_ref, first)
    last_even, last_odd = load_pair(depth_ref, momentum_ref, last)
    for i, tile in enumerate(pack([*first_even, *first_odd], 0, rim)):
        send_ref[i] = tile
    lane = lane_of((rows, lanes))
    for i, (head, tail) in enumerate(zip([*first_even, *first_odd], [*last_even, *last_odd])):
        if edge_ref.shape[0] == 1:
            edge_ref[0, i] = jnp.where(lane < 2 * rim, head, pltpu.roll(tail, 4 * rim, 1))
        else:
            edge_ref[0, i] = head
            edge_ref[1, i] = pltpu.roll(tail, lanes // 2, 1)

    out_ref[...] = jnp.zeros(out_ref.shape, out_ref.dtype)
    loaded = [load_pair(depth_ref, momentum_ref, slot) for slot in slots]
    initial = [[[pair[parity][i] for pair in loaded] for i in range(3)] for parity in range(2)]
    own = lax.axis_index("tm")
    for n in range(slices):

        @pl.when(own == n)
        def _(n=n):
            ending = Parareal(Scheme((rows, lanes), True), initial).end(KITER, n)
            for k, slot in enumerate(slots):

                @pl.when(k < count)
                def _(k=k, slot=slot):
                    for parity in range(2):
                        for i in range(3):
                            out_ref[slot, i, pl.ds(parity, rows, stride=2), :] = ending[parity][i][k]


def edge_kernel(rim, slices, inner_ref, edge_ref, west_ref, east_ref, live_ref, near_ref, out_ref):
    blocks, _, height, lanes = inner_ref.shape
    rows = height // 2
    tiles = edge_ref.shape[0]
    lane = lane_of((rows, lanes))
    first, last = run_of(live_ref, near_ref, blocks)
    pieces = []
    for i in range(6):
        west = unpack(west_ref, i, lanes - rim, rim)
        if tiles == 1:
            east = unpack(east_ref, i, 4 * rim, rim)
            own = jnp.where(lane < 4 * rim, edge_ref[0, i], east)
            pieces.append([jnp.where(lane < lanes - rim, own, west)])
        else:
            east = unpack(east_ref, i, lanes // 2, rim)
            pieces.append(
                [
                    jnp.where(lane < lanes - rim, edge_ref[0, i], west),
                    jnp.where(lane < lanes // 2, edge_ref[1, i], east),
                ]
            )
    initial = [pieces[:3], pieces[3:]]
    out_ref[...] = inner_ref[...]
    own = lax.axis_index("tm")
    for n in range(slices):

        @pl.when(own == n)
        def _(n=n):
            ending = Parareal(Scheme((rows, lanes), False), initial).end(KITER, n)
            turn = -4 * rim if tiles == 1 else lanes // 2
            for parity in range(2):
                for i in range(3):
                    rows_at = pl.ds(parity, rows, stride=2)
                    result = ending[parity][i]
                    out_ref[first, i, rows_at, :] = jnp.where(lane < rim, result[0], out_ref[first, i, rows_at, :])
                    tail = pltpu.roll(result[-1], turn % lanes, 1)
                    out_ref[last, i, rows_at, :] = jnp.where(
                        lane >= lanes - rim, tail, out_ref[last, i, rows_at, :]
                    )


def local(water_depth, momentum, slot_live, neighbours):
    blocks, height, lanes = water_depth.shape
    rows = height // 2
    slices = lax.axis_size("tm")
    owners = lax.axis_size("space")
    rim = 2 * (slices - 1) + 2 * SUB * KITER - 2
    strip = jax.ShapeDtypeStruct((-(-6 // (lanes // rim)), rows, lanes), jnp.float32)
    edge = jax.ShapeDtypeStruct((1 if 6 * rim <= lanes else 2, 6, rows, lanes), jnp.float32)
    whole = jax.ShapeDtypeStruct((blocks, 3, height, lanes), jnp.float32)
    vmem = pl.BlockSpec(memory_space=pltpu.VMEM)
    smem = pl.BlockSpec(memory_space=pltpu.SMEM)
    up = [(i, (i + 1) % owners) for i in range(owners)]
    down = [(j, i) for i, j in up]

    params = pltpu.CompilerParams(vmem_limit_bytes=16 * 1024 * 1024)
    east_rim = pl.pallas_call(
        functools.partial(send_east_kernel, rim),
        out_shape=strip,
        in_specs=[vmem, vmem, smem, smem],
        out_specs=vmem,
        compiler_params=params,
        name="send_east",
    )(water_depth, momentum, slot_live, neighbours)
    from_west = lax.ppermute(east_rim, "space", up)
    inner, west_rim, edges = pl.pallas_call(
        functools.partial(interior_kernel, rim, slices),
        out_shape=(whole, strip, edge),
        in_specs=[vmem, vmem, smem, smem],
        out_specs=(vmem, vmem, vmem),
        compiler_params=params,
        cost_estimate=pl.CostEstimate(flops=20_000_000, bytes_accessed=200_000, transcendentals=0),
        name="interior",
    )(water_depth, momentum, slot_live, neighbours)
    from_east = lax.ppermute(west_rim, "space", down)
    ends = pl.pallas_call(
        functools.partial(edge_kernel, rim, slices),
        out_shape=whole,
        in_specs=[vmem, vmem, vmem, vmem, smem, smem],
        out_specs=vmem,
        compiler_params=params,
        name="edges",
    )(inner, edges, from_west, from_east, slot_live, neighbours)
    return ends[None]


def solution(mesh):
    placed = (P("space", None, None), P("space", None, None, None), P("space"), P("space", None))
    return jax.shard_map(
        local,
        mesh=mesh,
        in_specs=placed,
        out_specs=P("tm", "space", None, None, None),
        check_vma=False,
    )
```

```python
import functools

import jax
import jax.numpy as jnp
from jax import lax
from jax.experimental import pallas as pl
from jax.experimental.pallas import tpu as pltpu
from jax.sharding import PartitionSpec as P

SUB = 3
KITER = 2
TIME_STEP = 0.15


def lane_of(shape):
    return lax.broadcasted_iota(jnp.int32, shape, 1)


def row_of(shape):
    return lax.broadcasted_iota(jnp.int32, shape, 0)


class Scheme:
    def __init__(self, shape, linked, mode):
        self.rows, self.lanes = shape
        self.linked = linked
        self.mode = mode
        lane, row = lane_of(shape), row_of(shape)
        self.is_first_lane = lane == 0
        self.is_last_lane = lane == self.lanes - 1
        self.is_first_row = row == 0
        self.is_last_row = row == self.rows - 1

    def east(self, tiles):
        rolled = [pltpu.roll(tile, self.lanes - 1, 1) for tile in tiles]
        if not self.linked:
            return rolled
        return [
            jnp.where(self.is_last_lane, rolled[k + 1], rolled[k]) if k + 1 < len(rolled) else rolled[k]
            for k in range(len(rolled))
        ]

    def west(self, tiles):
        rolled = [pltpu.roll(tile, 1, 1) for tile in tiles]
        if not self.linked:
            return rolled
        return [jnp.where(self.is_first_lane, rolled[k - 1], rolled[k]) if k else rolled[k] for k in range(len(rolled))]

    def above(self, tile):
        return pltpu.roll(tile, self.rows - 1, 0)

    def below(self, tile):
        return pltpu.roll(tile, 1, 0)

    @staticmethod
    def derive(h, hu, hv, needed=(3, 4, 5, 6, 7)):
        root = lax.rsqrt(h)
        celerity = h * root
        inverse = root * root
        u = hu * inverse
        p = (0.5 * h) * h
        part = [h, hu, hv, hu * u + p, hv * u, None, jnp.abs(u) + celerity, None]
        if 5 in needed:
            q = hv * inverse
            part[5] = hv * q + p
            part[7] = jnp.abs(q) + celerity
        return part

    def derived(self, state):
        return [self.derive(h, hu, hv) for h, hu, hv in zip(*state)]

    def moved(self, parts, shift):
        if self.mode == "fields":
            states = zip(*(shift([part[i] for part in parts]) for i in (0, 1, 2)))
            return [self.derive(h, hu, hv, ()) for h, hu, hv in states]
        columns = {i: shift([part[i] for part in parts]) for i in (0, 1, 2, 3, 4, 6)}
        return [[columns[i][k] if i in columns else None for i in range(8)] for k in range(len(parts))]

    @staticmethod
    def faces_along(lower, upper):
        bound = jnp.maximum(lower[6], upper[6])
        return [(lower[f] + upper[f]) - bound * (upper[v] - lower[v]) for v, f in ((0, 1), (1, 3), (2, 4))]

    def along(self, parts):
        east = [self.faces_along(a, b) for a, b in zip(parts, self.moved(parts, self.east))]
        if self.mode == "serial":
            west = list(zip(*(self.west([face[i] for face in east]) for i in range(3))))
        else:
            west = [self.faces_along(a, b) for a, b in zip(self.moved(parts, self.west), parts)]
        return [[e[i] - w[i] for e, w in zip(east, west)] for i in range(3)]

    @staticmethod
    def cross(lower, upper):
        bound = jnp.maximum(lower[7], upper[7])
        return [
            (lower[f] + upper[f]) - bound * (upper[v] - lower[v]) for v, f in ((0, 2), (1, 4), (2, 5))
        ]

    def upper_faces(self, top, raised):
        faces = self.cross(top, raised)
        wall = 2.0 * (top[5] + top[7] * top[2])
        return [
            jnp.where(self.is_last_row, 0.0, faces[0]),
            jnp.where(self.is_last_row, 0.0, faces[1]),
            jnp.where(self.is_last_row, wall, faces[2]),
        ]

    def lower_faces(self, bottom, faces):
        wall = 2.0 * (bottom[5] - bottom[7] * bottom[2])
        lowered = [self.below(face) for face in faces]
        return [lowered[0], lowered[1], jnp.where(self.is_first_row, wall, lowered[2])]

    def raise_up(self, part):
        return [self.above(part[i]) if i in (0, 1, 2, 4, 5, 7) else None for i in range(8)]

    def fine_change(self, even, odd):
        even_parts, odd_parts = self.derived(even), self.derived(odd)
        even_x, odd_x = self.along(even_parts), self.along(odd_parts)
        even_out, odd_out = [[], [], []], [[], [], []]
        for k, (a, b) in enumerate(zip(even_parts, odd_parts)):
            inner = self.cross(a, b)
            upper = self.upper_faces(b, self.raise_up(a))
            lower = self.lower_faces(a, upper)
            for i in range(3):
                even_out[i].append(even_x[i][k] + (inner[i] - lower[i]))
                odd_out[i].append(odd_x[i][k] + (upper[i] - inner[i]))
        return even_out, odd_out

    def coarse_change(self, state):
        parts = self.derived(state)
        x = self.along(parts)
        out = [[], [], []]
        for k, a in enumerate(parts):
            upper = self.upper_faces(a, self.raise_up(a))
            lower = self.lower_faces(a, upper)
            for i in range(3):
                out[i].append(SUB * x[i][k] + (upper[i] - lower[i]))
        return out

    @staticmethod
    def plus(a, b):
        return [[s + t for s, t in zip(u, v)] for u, v in zip(a, b)]

    @staticmethod
    def minus(a, b):
        return [[s - t for s, t in zip(u, v)] for u, v in zip(a, b)]

    @staticmethod
    def times(a, factor):
        return [[factor * s for s in u] for u in a]

    def heun(self, states, change):
        start = change(*states)
        first = [self.minus(s, self.times(c, 0.5 * TIME_STEP)) for s, c in zip(states, start)]
        following = change(*first)
        return [
            self.minus(s, self.times(self.plus(c, d), 0.25 * TIME_STEP)) for s, c, d in zip(states, start, following)
        ]

    def coarse(self, state):
        return self.heun([state], lambda one: [self.coarse_change(one)])[0]

    def fine(self, pair):
        for _ in range(SUB):
            pair = self.heun(pair, self.fine_change)
        return pair

    def restrict(self, pair):
        return self.times(self.plus(pair[0], pair[1]), 0.5)


class Parareal:
    def __init__(self, scheme, initial):
        self.scheme = scheme
        self.initial = initial
        self.known = {}

    def memo(self, key, build):
        if key not in self.known:
            self.known[key] = build()
        return self.known[key]

    def coarse_state(self, sweep, n):
        sweep = min(sweep, n)

        def build():
            s = self.scheme
            if n == 0:
                return s.restrict(self.initial)
            stepped = self.coarse_step(sweep, n - 1)
            if sweep == 0:
                return stepped
            correction = s.minus(s.restrict(self.fine_run(sweep, n - 1)), self.coarse_step(sweep - 1, n - 1))
            return s.plus(stepped, correction)

        return self.memo(("c", sweep, n), build)

    def coarse_step(self, sweep, n):
        sweep = min(sweep, n)
        return self.memo(("k", sweep, n), lambda: self.scheme.coarse(self.coarse_state(sweep, n)))

    def fine_run(self, sweep, n):
        sweep = 1 if n == 0 else sweep

        def build():
            if n == 0:
                start = self.initial
            elif sweep == 1:
                state = self.coarse_state(0, n)
                start = [state, state]
            else:
                start = self.end(sweep - 1, n - 1)
            return self.scheme.fine(start)

        return self.memo(("f", sweep, n), build)

    def end(self, sweep, n):
        def build():
            s = self.scheme
            refined = self.fine_run(sweep, n)
            renewed, previous = self.coarse_step(sweep, n), self.coarse_step(sweep - 1, n)
            return [s.minus(s.plus(renewed, part), previous) for part in refined]

        return self.memo(("e", sweep, n), build)


def run_of(live_ref, near_ref, blocks):
    slot = jnp.int32(0)
    count = jnp.int32(0)
    for k in range(blocks):
        slot = jnp.where((live_ref[k] == 1) & (near_ref[0, k] == blocks), k, slot)
        count += live_ref[k]
    slots = [slot]
    for _ in range(blocks - 1):
        following = near_ref[1, slots[-1]]
        slots.append(jnp.where(following < blocks, following, slots[-1]))
    return slots, count


def load_fields(depth_ref, momentum_ref, slot):
    rows = depth_ref.shape[1] // 2
    return [
        ref[pl.ds(parity, rows, stride=2), :]
        for parity in range(2)
        for ref in (depth_ref.at[slot], momentum_ref.at[slot, 0], momentum_ref.at[slot, 1])
    ]


def pack(pieces, start, rim):
    rows, lanes = pieces[0].shape
    lane = lane_of((rows, lanes))
    per_tile = lanes // rim
    tiles = []
    for i, piece in enumerate(pieces):
        place = (i % per_tile) * rim
        moved = pltpu.roll(piece, (place - start) % lanes, 1)
        if place == 0:
            tiles.append(moved)
        else:
            tiles[-1] = jnp.where(lane >= place, moved, tiles[-1])
    return tiles


def unpack(packed_ref, index, place, rim):
    lanes = packed_ref.shape[2]
    per_tile = lanes // rim
    source = (index % per_tile) * rim
    return pltpu.roll(packed_ref[index // per_tile], (place - source) % lanes, 1)


def send_kernel(
    rim, depth_hbm, momentum_hbm, live_hbm, near_hbm, east_ref, west_ref, run_ref, edge_ref, place_ref,
    depth_ref, momentum_ref, live_ref, near_ref, sems,
):
    copies = [
        pltpu.make_async_copy(source, target, sems.at[i])
        for i, (source, target) in enumerate(
            ((live_hbm, live_ref), (near_hbm, near_ref), (depth_hbm, depth_ref), (momentum_hbm, momentum_ref))
        )
    ]
    for copy in copies:
        copy.start()
    for copy in copies:
        copy.wait()
    blocks, height, lanes = depth_ref.shape
    rows = height // 2
    slots, count = run_of(live_ref, near_ref, blocks)
    tiles = [load_fields(depth_ref, momentum_ref, slot) for slot in slots]
    first, last = tiles[0], tiles[-1]
    for i, tile in enumerate(pack(last, lanes - rim, rim)):
        east_ref[i] = tile
    for i, tile in enumerate(pack(first, 0, rim)):
        west_ref[i] = tile
    for k, fields in enumerate(tiles):
        for i in range(6):
            run_ref[k, i] = fields[i]
        place_ref[k] = jnp.full((rows, lanes), jnp.where(k < count, slots[k], -1), jnp.int32)
    lane = lane_of((rows, lanes))
    for i, (head, tail) in enumerate(zip(first, last)):
        if edge_ref.shape[0] == 1:
            edge_ref[0, i] = jnp.where(lane < 2 * rim, head, pltpu.roll(tail, 4 * rim, 1))
        else:
            edge_ref[0, i] = head
            edge_ref[1, i] = pltpu.roll(tail, lanes // 2, 1)


def as_initial(tiles):
    return [[[tile[3 * parity + i] for tile in tiles] for i in range(3)] for parity in range(2)]


def interior_kernel(slices, run_ref, out_ref):
    blocks, _, rows, lanes = run_ref.shape
    own = lax.axis_index("tm")
    for n in range(slices):

        @pl.when(own == n)
        def _(n=n):
            tiles = [[run_ref[k, i] for i in range(6)] for k in range(blocks)]
            ending = Parareal(Scheme((rows, lanes), True, "serial"), as_initial(tiles)).end(KITER, n)
            for k in range(blocks):
                for i in range(6):
                    out_ref[k, i] = ending[i // 3][i % 3][k]


def edge_kernel(rim, slices, inner_ref, edge_ref, west_ref, east_ref, place_ref, out_ref):
    blocks, _, rows, lanes = inner_ref.shape
    edges = edge_ref.shape[0]
    own = lax.axis_index("tm")
    for n in range(slices):

        @pl.when(own == n)
        def _(n=n):
            lane = lane_of((rows, lanes))
            tiles = [[] for _ in range(edges)]
            for i in range(6):
                west = unpack(west_ref, i, lanes - rim, rim)
                east_start = 4 * rim if edges == 1 else lanes // 2
                east = unpack(east_ref, i, east_start, rim)
                tiles[-1].append(jnp.where(lane < east_start, edge_ref[edges - 1, i], east))
                tiles[0][i:] = [jnp.where(lane < lanes - rim, tiles[0][i] if edges == 1 else edge_ref[0, i], west)]
            ending = Parareal(Scheme((rows, lanes), False, "both"), as_initial(tiles)).end(KITER, n)
            places = [place_ref[k] for k in range(blocks)]
            lasts = [
                (places[k] >= 0) & (places[k + 1] < 0) if k + 1 < blocks else places[k] >= 0 for k in range(blocks)
            ]
            for i in range(6):
                result = ending[i // 3][i % 3]
                tail = pltpu.roll(result[-1], (-4 * rim if edges == 1 else lanes // 2) % lanes, 1)
                merged = []
                for k in range(blocks):
                    tile = jnp.where(lasts[k] & (lane >= lanes - rim), tail, inner_ref[k, i])
                    merged.append(jnp.where(lane < rim, result[0], tile) if k == 0 else tile)
                for slot in range(blocks):
                    chosen = jnp.zeros((rows, lanes), jnp.float32)
                    for k in range(blocks):
                        chosen = jnp.where(places[k] == slot, merged[k], chosen)
                    out_ref[slot, i % 3, pl.ds(i // 3, rows, stride=2), :] = chosen


def local(water_depth, momentum, slot_live, neighbours):
    blocks, height, lanes = water_depth.shape
    rows = height // 2
    slices = lax.axis_size("tm")
    owners = lax.axis_size("space")
    rim = 2 * (slices - 1) + 2 * SUB * KITER - 2
    strip = jax.ShapeDtypeStruct((-(-6 // (lanes // rim)), rows, lanes), jnp.float32)
    edge = jax.ShapeDtypeStruct((1 if 6 * rim <= lanes else 2, 6, rows, lanes), jnp.float32)
    run = jax.ShapeDtypeStruct((blocks, 6, rows, lanes), jnp.float32)
    place = jax.ShapeDtypeStruct((blocks, rows, lanes), jnp.int32)
    whole = jax.ShapeDtypeStruct((blocks, 3, height, lanes), jnp.float32)
    vmem = pl.BlockSpec(memory_space=pltpu.VMEM)
    hbm = pl.BlockSpec(memory_space=pltpu.HBM)
    up = [(i, (i + 1) % owners) for i in range(owners)]
    down = [(j, i) for i, j in up]

    params = pltpu.CompilerParams(vmem_limit_bytes=16 * 1024 * 1024)
    east_rim, west_rim, tiles, edges, places = pl.pallas_call(
        functools.partial(send_kernel, rim),
        out_shape=(strip, strip, run, edge, place),
        in_specs=[hbm] * 4,
        out_specs=(vmem,) * 5,
        scratch_shapes=[
            pltpu.VMEM(water_depth.shape, jnp.float32),
            pltpu.VMEM(momentum.shape, jnp.float32),
            pltpu.SMEM(slot_live.shape, jnp.int32),
            pltpu.SMEM(neighbours.shape[::-1], jnp.int32),
            pltpu.SemaphoreType.DMA((4,)),
        ],
        compiler_params=params,
        name="send",
    )(*(pltpu.with_memory_space_constraint(x, pltpu.HBM) for x in (water_depth, momentum, slot_live, neighbours.T)))
    from_west = lax.ppermute(east_rim, "space", up)
    from_east = lax.ppermute(west_rim, "space", down)
    inner = pl.pallas_call(
        functools.partial(interior_kernel, slices),
        out_shape=run,
        in_specs=[vmem],
        out_specs=vmem,
        compiler_params=params,
        cost_estimate=pl.CostEstimate(flops=20_000_000, bytes_accessed=200_000, transcendentals=0),
        name="interior",
    )(tiles)
    ends = pl.pallas_call(
        functools.partial(edge_kernel, rim, slices),
        out_shape=whole,
        in_specs=[vmem] * 5,
        out_specs=vmem,
        compiler_params=params,
        name="edges",
    )(inner, edges, from_west, from_east, places)
    return ends[None]


def solution(mesh):
    placed = (P("space", None, None), P("space", None, None, None), P("space"), P("space", None))
    return jax.shard_map(
        local,
        mesh=mesh,
        in_specs=placed,
        out_specs=P("tm", "space", None, None, None),
        check_vma=False,
    )
```

```python
import functools

import jax
import jax.numpy as jnp
from jax import lax
from jax.experimental import pallas as pl
from jax.experimental.pallas import tpu as pltpu
from jax.sharding import PartitionSpec as P

SUB = 3
KITER = 2
TIME_STEP = 0.15


def lane_of(shape):
    return lax.broadcasted_iota(jnp.int32, shape, 1)


def row_of(shape):
    return lax.broadcasted_iota(jnp.int32, shape, 0)


class Scheme:
    def __init__(self, shape, linked, fine_fast, coarse_fast):
        self.rows, self.lanes = shape
        self.linked = linked
        self.fine_fast = fine_fast
        self.coarse_fast = coarse_fast
        lane, row = lane_of(shape), row_of(shape)
        self.is_first_lane = lane == 0
        self.is_last_lane = lane == self.lanes - 1
        self.is_first_row = row == 0
        self.is_last_row = row == self.rows - 1

    def east(self, tiles):
        rolled = [pltpu.roll(tile, self.lanes - 1, 1) for tile in tiles]
        if not self.linked:
            return rolled
        return [
            jnp.where(self.is_last_lane, rolled[k + 1], rolled[k]) if k + 1 < len(rolled) else rolled[k]
            for k in range(len(rolled))
        ]

    def west(self, tiles):
        rolled = [pltpu.roll(tile, 1, 1) for tile in tiles]
        if not self.linked:
            return rolled
        return [jnp.where(self.is_first_lane, rolled[k - 1], rolled[k]) if k else rolled[k] for k in range(len(rolled))]

    def above(self, tile):
        return pltpu.roll(tile, self.rows - 1, 0)

    def below(self, tile):
        return pltpu.roll(tile, 1, 0)

    @staticmethod
    def derive(h, hu, hv, needed=(3, 4, 5, 6, 7)):
        root = lax.rsqrt(h)
        celerity = h * root
        inverse = root * root
        u = hu * inverse
        p = (0.5 * h) * h
        part = [h, hu, hv, hu * u + p, hv * u, None, jnp.abs(u) + celerity, None]
        if 5 in needed:
            q = hv * inverse
            part[5] = hv * q + p
            part[7] = jnp.abs(q) + celerity
        return part

    def derived(self, state):
        return [self.derive(h, hu, hv) for h, hu, hv in zip(*state)]

    def moved(self, parts, shift):
        states = zip(*(shift([part[i] for part in parts]) for i in (0, 1, 2)))
        return [self.derive(h, hu, hv, ()) for h, hu, hv in states]

    @staticmethod
    def faces_along(lower, upper):
        bound = jnp.maximum(lower[6], upper[6])
        return [(lower[f] + upper[f]) - bound * (upper[v] - lower[v]) for v, f in ((0, 1), (1, 3), (2, 4))]

    def along(self, parts, latency):
        east = [self.faces_along(a, b) for a, b in zip(parts, self.moved(parts, self.east))]
        if not latency:
            west = list(zip(*(self.west([face[i] for face in east]) for i in range(3))))
        else:
            west = [self.faces_along(a, b) for a, b in zip(self.moved(parts, self.west), parts)]
        return [[e[i] - w[i] for e, w in zip(east, west)] for i in range(3)]

    @staticmethod
    def cross(lower, upper):
        bound = jnp.maximum(lower[7], upper[7])
        return [
            (lower[f] + upper[f]) - bound * (upper[v] - lower[v]) for v, f in ((0, 2), (1, 4), (2, 5))
        ]

    def upper_faces(self, top, raised):
        faces = self.cross(top, raised)
        wall = 2.0 * (top[5] + top[7] * top[2])
        return [
            jnp.where(self.is_last_row, 0.0, faces[0]),
            jnp.where(self.is_last_row, 0.0, faces[1]),
            jnp.where(self.is_last_row, wall, faces[2]),
        ]

    def lower_faces(self, bottom, faces):
        wall = 2.0 * (bottom[5] - bottom[7] * bottom[2])
        lowered = [self.below(face) for face in faces]
        return [lowered[0], lowered[1], jnp.where(self.is_first_row, wall, lowered[2])]

    def raise_up(self, part):
        return [self.above(part[i]) if i in (0, 1, 2, 4, 5, 7) else None for i in range(8)]

    def fine_change(self, even, odd, latency):
        even_parts, odd_parts = self.derived(even), self.derived(odd)
        even_x, odd_x = self.along(even_parts, latency), self.along(odd_parts, latency)
        even_out, odd_out = [[], [], []], [[], [], []]
        for k, (a, b) in enumerate(zip(even_parts, odd_parts)):
            inner = self.cross(a, b)
            upper = self.upper_faces(b, self.raise_up(a))
            lower = self.lower_faces(a, upper)
            for i in range(3):
                even_out[i].append(even_x[i][k] + (inner[i] - lower[i]))
                odd_out[i].append(odd_x[i][k] + (upper[i] - inner[i]))
        return even_out, odd_out

    def coarse_change(self, state):
        parts = self.derived(state)
        x = self.along(parts, self.coarse_fast)
        out = [[], [], []]
        for k, a in enumerate(parts):
            upper = self.upper_faces(a, self.raise_up(a))
            lower = self.lower_faces(a, upper)
            for i in range(3):
                out[i].append(SUB * x[i][k] + (upper[i] - lower[i]))
        return out

    @staticmethod
    def plus(a, b):
        return [[s + t for s, t in zip(u, v)] for u, v in zip(a, b)]

    @staticmethod
    def minus(a, b):
        return [[s - t for s, t in zip(u, v)] for u, v in zip(a, b)]

    @staticmethod
    def times(a, factor):
        return [[factor * s for s in u] for u in a]

    def heun(self, states, change):
        start = change(*states)
        first = [self.minus(s, self.times(c, 0.5 * TIME_STEP)) for s, c in zip(states, start)]
        following = change(*first)
        return [
            self.minus(s, self.times(self.plus(c, d), 0.25 * TIME_STEP)) for s, c, d in zip(states, start, following)
        ]

    def coarse(self, state):
        return self.heun([state], lambda one: [self.coarse_change(one)])[0]

    def fine(self, pair, name):
        latency = self.fine_fast == "all" or name in self.fine_fast
        for _ in range(SUB):
            pair = self.heun(pair, lambda even, odd: self.fine_change(even, odd, latency))
        return pair

    def restrict(self, pair):
        return self.times(self.plus(pair[0], pair[1]), 0.5)


class Parareal:
    def __init__(self, scheme, initial):
        self.scheme = scheme
        self.initial = initial
        self.known = {}

    def memo(self, key, build):
        if key not in self.known:
            self.known[key] = build()
        return self.known[key]

    def coarse_state(self, sweep, n):
        sweep = min(sweep, n)

        def build():
            s = self.scheme
            if n == 0:
                return s.restrict(self.initial)
            stepped = self.coarse_step(sweep, n - 1)
            if sweep == 0:
                return stepped
            correction = s.minus(s.restrict(self.fine_run(sweep, n - 1)), self.coarse_step(sweep - 1, n - 1))
            return s.plus(stepped, correction)

        return self.memo(("c", sweep, n), build)

    def coarse_step(self, sweep, n):
        sweep = min(sweep, n)
        return self.memo(("k", sweep, n), lambda: self.scheme.coarse(self.coarse_state(sweep, n)))

    def fine_run(self, sweep, n):
        sweep = 1 if n == 0 else sweep

        def build():
            if n == 0:
                start = self.initial
            elif sweep == 1:
                state = self.coarse_state(0, n)
                start = [state, state]
            else:
                start = self.end(sweep - 1, n - 1)
            return self.scheme.fine(start, (sweep, n))

        return self.memo(("f", sweep, n), build)

    def end(self, sweep, n):
        def build():
            s = self.scheme
            refined = self.fine_run(sweep, n)
            renewed, previous = self.coarse_step(sweep, n), self.coarse_step(sweep - 1, n)
            return [s.minus(s.plus(renewed, part), previous) for part in refined]

        return self.memo(("e", sweep, n), build)


def run_of(live_ref, near_ref, blocks):
    slot = jnp.int32(0)
    count = jnp.int32(0)
    for k in range(blocks):
        slot = jnp.where((live_ref[k] == 1) & (near_ref[0, k] == blocks), k, slot)
        count += live_ref[k]
    slots = [slot]
    for _ in range(blocks - 1):
        following = near_ref[1, slots[-1]]
        slots.append(jnp.where(following < blocks, following, slots[-1]))
    return slots, count


def load_fields(depth_ref, momentum_ref, slot):
    rows = depth_ref.shape[1] // 2
    return [
        ref[pl.ds(parity, rows, stride=2), :]
        for parity in range(2)
        for ref in (depth_ref.at[slot], momentum_ref.at[slot, 0], momentum_ref.at[slot, 1])
    ]


def pack(pieces, start, rim):
    rows, lanes = pieces[0].shape
    lane = lane_of((rows, lanes))
    per_tile = lanes // rim
    tiles = []
    for i, piece in enumerate(pieces):
        place = (i % per_tile) * rim
        moved = pltpu.roll(piece, (place - start) % lanes, 1)
        if place == 0:
            tiles.append(moved)
        else:
            tiles[-1] = jnp.where(lane >= place, moved, tiles[-1])
    return tiles


def unpack(packed_ref, index, place, rim):
    lanes = packed_ref.shape[2]
    per_tile = lanes // rim
    source = (index % per_tile) * rim
    return pltpu.roll(packed_ref[index // per_tile], (place - source) % lanes, 1)


def send_kernel(
    rim, depth_hbm, momentum_hbm, live_hbm, near_hbm, east_ref, west_ref, run_ref, edge_ref, place_ref,
    depth_ref, momentum_ref, live_ref, near_ref, sems,
):
    copies = [
        pltpu.make_async_copy(source, target, sems.at[i])
        for i, (source, target) in enumerate(
            ((live_hbm, live_ref), (near_hbm, near_ref), (depth_hbm, depth_ref), (momentum_hbm, momentum_ref))
        )
    ]
    for copy in copies:
        copy.start()
    for copy in copies:
        copy.wait()
    blocks, height, lanes = depth_ref.shape
    rows = height // 2
    slots, count = run_of(live_ref, near_ref, blocks)
    tiles = [load_fields(depth_ref, momentum_ref, slot) for slot in slots]
    first, last = tiles[0], tiles[-1]
    for i, tile in enumerate(pack(last, lanes - rim, rim)):
        east_ref[i] = tile
    for i, tile in enumerate(pack(first, 0, rim)):
        west_ref[i] = tile
    for k, fields in enumerate(tiles):
        for i in range(6):
            run_ref[k, i] = fields[i]
        place_ref[k] = jnp.full((rows, lanes), jnp.where(k < count, slots[k], -1), jnp.int32)
    place_ref[blocks] = jnp.full((rows, lanes), count, jnp.int32)
    lane = lane_of((rows, lanes))
    for i, (head, tail) in enumerate(zip(first, last)):
        if edge_ref.shape[0] == 1:
            edge_ref[0, i] = jnp.where(lane < 2 * rim, head, pltpu.roll(tail, 4 * rim, 1))
        else:
            edge_ref[0, i] = head
            edge_ref[1, i] = pltpu.roll(tail, lanes // 2, 1)


def as_initial(tiles):
    return [[[tile[3 * parity + i] for tile in tiles] for i in range(3)] for parity in range(2)]


def interior_kernel(slices, run_ref, place_ref, out_ref):
    blocks, _, rows, lanes = run_ref.shape
    own = lax.axis_index("tm")
    count = place_ref[blocks][0, 0]
    for n in range(slices):
        for length in range(1, blocks + 1):

            @pl.when((own == n) & (count == length))
            def _(n=n, length=length):
                tiles = [[run_ref[k, i] for i in range(6)] for k in range(length)]
                fast = length < blocks or n < 2
                scheme = Scheme((rows, lanes), True, "all" if fast else (), True)
                ending = Parareal(scheme, as_initial(tiles)).end(KITER, n)
                for k in range(length):
                    for i in range(6):
                        out_ref[k, i] = ending[i // 3][i % 3][k]


def edge_kernel(rim, slices, inner_ref, edge_ref, west_ref, east_ref, place_ref, out_ref):
    blocks, _, rows, lanes = inner_ref.shape
    edges = edge_ref.shape[0]
    own = lax.axis_index("tm")
    for n in range(slices):

        @pl.when(own == n)
        def _(n=n):
            lane = lane_of((rows, lanes))
            tiles = [[] for _ in range(edges)]
            for i in range(6):
                west = unpack(west_ref, i, lanes - rim, rim)
                east_start = 4 * rim if edges == 1 else lanes // 2
                east = unpack(east_ref, i, east_start, rim)
                tiles[-1].append(jnp.where(lane < east_start, edge_ref[edges - 1, i], east))
                tiles[0][i:] = [jnp.where(lane < lanes - rim, tiles[0][i] if edges == 1 else edge_ref[0, i], west)]
            ending = Parareal(Scheme((rows, lanes), False, "all", True), as_initial(tiles)).end(KITER, n)
            places = [place_ref[k] for k in range(blocks)]
            lasts = [
                (places[k] >= 0) & (places[k + 1] < 0) if k + 1 < blocks else places[k] >= 0 for k in range(blocks)
            ]
            for i in range(6):
                result = ending[i // 3][i % 3]
                tail = pltpu.roll(result[-1], (-4 * rim if edges == 1 else lanes // 2) % lanes, 1)
                merged = []
                for k in range(blocks):
                    tile = jnp.where(lasts[k] & (lane >= lanes - rim), tail, inner_ref[k, i])
                    merged.append(jnp.where(lane < rim, result[0], tile) if k == 0 else tile)
                for slot in range(blocks):
                    chosen = jnp.zeros((rows, lanes), jnp.float32)
                    for k in range(blocks):
                        chosen = jnp.where(places[k] == slot, merged[k], chosen)
                    out_ref[slot, i % 3, pl.ds(i // 3, rows, stride=2), :] = chosen


def local(water_depth, momentum, slot_live, neighbours):
    blocks, height, lanes = water_depth.shape
    rows = height // 2
    slices = lax.axis_size("tm")
    owners = lax.axis_size("space")
    rim = 2 * (slices - 1) + 2 * SUB * KITER - 2
    strip = jax.ShapeDtypeStruct((-(-6 // (lanes // rim)), rows, lanes), jnp.float32)
    edge = jax.ShapeDtypeStruct((1 if 6 * rim <= lanes else 2, 6, rows, lanes), jnp.float32)
    run = jax.ShapeDtypeStruct((blocks, 6, rows, lanes), jnp.float32)
    place = jax.ShapeDtypeStruct((blocks + 1, rows, lanes), jnp.int32)
    whole = jax.ShapeDtypeStruct((blocks, 3, height, lanes), jnp.float32)
    vmem = pl.BlockSpec(memory_space=pltpu.VMEM)
    hbm = pl.BlockSpec(memory_space=pltpu.HBM)
    up = [(i, (i + 1) % owners) for i in range(owners)]
    down = [(j, i) for i, j in up]

    params = pltpu.CompilerParams(vmem_limit_bytes=16 * 1024 * 1024)
    east_rim, west_rim, tiles, edges, places = pl.pallas_call(
        functools.partial(send_kernel, rim),
        out_shape=(strip, strip, run, edge, place),
        in_specs=[hbm] * 4,
        out_specs=(vmem,) * 5,
        scratch_shapes=[
            pltpu.VMEM(water_depth.shape, jnp.float32),
            pltpu.VMEM(momentum.shape, jnp.float32),
            pltpu.SMEM(slot_live.shape, jnp.int32),
            pltpu.SMEM(neighbours.shape[::-1], jnp.int32),
            pltpu.SemaphoreType.DMA((4,)),
        ],
        compiler_params=params,
        name="send",
    )(*(pltpu.with_memory_space_constraint(x, pltpu.HBM) for x in (water_depth, momentum, slot_live, neighbours.T)))
    from_west = lax.ppermute(east_rim, "space", up)
    from_east = lax.ppermute(west_rim, "space", down)
    inner = pl.pallas_call(
        functools.partial(interior_kernel, slices),
        out_shape=run,
        in_specs=[vmem, vmem],
        out_specs=vmem,
        compiler_params=params,
        cost_estimate=pl.CostEstimate(flops=20_000_000, bytes_accessed=200_000, transcendentals=0),
        name="interior",
    )(tiles, places)
    ends = pl.pallas_call(
        functools.partial(edge_kernel, rim, slices),
        out_shape=whole,
        in_specs=[vmem] * 5,
        out_specs=vmem,
        compiler_params=params,
        name="edges",
    )(inner, edges, from_west, from_east, places)
    return ends[None]


def solution(mesh):
    placed = (P("space", None, None), P("space", None, None, None), P("space"), P("space", None))
    return jax.shard_map(
        local,
        mesh=mesh,
        in_specs=placed,
        out_specs=P("tm", "space", None, None, None),
        check_vma=False,
    )
```

```python
import functools

import jax
import jax.numpy as jnp
from jax import lax
from jax.experimental import pallas as pl
from jax.experimental.pallas import tpu as pltpu
from jax.sharding import PartitionSpec as P

SUB = 3
KITER = 2
TIME_STEP = 0.15
SHORT_SLICES = 2
SPLIT_SLICES = 4


def lane_of(shape):
    return lax.broadcasted_iota(jnp.int32, shape, 1)


def row_of(shape):
    return lax.broadcasted_iota(jnp.int32, shape, 0)


class Scheme:
    def __init__(self, shape, linked, fine_fast, coarse_fast):
        self.rows, self.lanes = shape
        self.linked = linked
        self.fine_fast = fine_fast
        self.coarse_fast = coarse_fast
        lane, row = lane_of(shape), row_of(shape)
        self.is_first_lane = lane == 0
        self.is_last_lane = lane == self.lanes - 1
        self.is_first_row = row == 0
        self.is_last_row = row == self.rows - 1

    def east(self, tiles):
        rolled = [pltpu.roll(tile, self.lanes - 1, 1) for tile in tiles]
        if not self.linked:
            return rolled
        return [
            jnp.where(self.is_last_lane, rolled[k + 1], rolled[k]) if k + 1 < len(rolled) else rolled[k]
            for k in range(len(rolled))
        ]

    def west(self, tiles):
        rolled = [pltpu.roll(tile, 1, 1) for tile in tiles]
        if not self.linked:
            return rolled
        return [jnp.where(self.is_first_lane, rolled[k - 1], rolled[k]) if k else rolled[k] for k in range(len(rolled))]

    def above(self, tile):
        return pltpu.roll(tile, self.rows - 1, 0)

    def below(self, tile):
        return pltpu.roll(tile, 1, 0)

    @staticmethod
    def derive(h, hu, hv, needed=(3, 4, 5, 6, 7)):
        root = lax.rsqrt(h)
        celerity = h * root
        inverse = root * root
        u = hu * inverse
        p = (0.5 * h) * h
        part = [h, hu, hv, hu * u + p, hv * u, None, jnp.abs(u) + celerity, None]
        if 5 in needed:
            q = hv * inverse
            part[5] = hv * q + p
            part[7] = jnp.abs(q) + celerity
        return part

    def derived(self, state):
        return [self.derive(h, hu, hv) for h, hu, hv in zip(*state)]

    def moved(self, parts, shift):
        states = zip(*(shift([part[i] for part in parts]) for i in (0, 1, 2)))
        return [self.derive(h, hu, hv, ()) for h, hu, hv in states]

    @staticmethod
    def faces_along(lower, upper):
        bound = jnp.maximum(lower[6], upper[6])
        return [(lower[f] + upper[f]) - bound * (upper[v] - lower[v]) for v, f in ((0, 1), (1, 3), (2, 4))]

    def along(self, parts, latency):
        east = [self.faces_along(a, b) for a, b in zip(parts, self.moved(parts, self.east))]
        if not latency:
            west = list(zip(*(self.west([face[i] for face in east]) for i in range(3))))
        else:
            west = [self.faces_along(a, b) for a, b in zip(self.moved(parts, self.west), parts)]
        return [[e[i] - w[i] for e, w in zip(east, west)] for i in range(3)]

    @staticmethod
    def cross(lower, upper):
        bound = jnp.maximum(lower[7], upper[7])
        return [
            (lower[f] + upper[f]) - bound * (upper[v] - lower[v]) for v, f in ((0, 2), (1, 4), (2, 5))
        ]

    def upper_faces(self, top, raised):
        faces = self.cross(top, raised)
        wall = 2.0 * (top[5] + top[7] * top[2])
        return [
            jnp.where(self.is_last_row, 0.0, faces[0]),
            jnp.where(self.is_last_row, 0.0, faces[1]),
            jnp.where(self.is_last_row, wall, faces[2]),
        ]

    def lower_faces(self, bottom, faces):
        wall = 2.0 * (bottom[5] - bottom[7] * bottom[2])
        lowered = [self.below(face) for face in faces]
        return [lowered[0], lowered[1], jnp.where(self.is_first_row, wall, lowered[2])]

    def raise_up(self, part):
        return [self.above(part[i]) if i in (0, 1, 2, 4, 5, 7) else None for i in range(8)]

    def fine_change(self, even, odd, latency):
        even_parts, odd_parts = self.derived(even), self.derived(odd)
        even_x, odd_x = self.along(even_parts, latency), self.along(odd_parts, latency)
        even_out, odd_out = [[], [], []], [[], [], []]
        for k, (a, b) in enumerate(zip(even_parts, odd_parts)):
            inner = self.cross(a, b)
            upper = self.upper_faces(b, self.raise_up(a))
            lower = self.lower_faces(a, upper)
            for i in range(3):
                even_out[i].append(even_x[i][k] + (inner[i] - lower[i]))
                odd_out[i].append(odd_x[i][k] + (upper[i] - inner[i]))
        return even_out, odd_out

    def coarse_change(self, state):
        parts = self.derived(state)
        x = self.along(parts, self.coarse_fast)
        out = [[], [], []]
        for k, a in enumerate(parts):
            upper = self.upper_faces(a, self.raise_up(a))
            lower = self.lower_faces(a, upper)
            for i in range(3):
                out[i].append(SUB * x[i][k] + (upper[i] - lower[i]))
        return out

    @staticmethod
    def plus(a, b):
        return [[s + t for s, t in zip(u, v)] for u, v in zip(a, b)]

    @staticmethod
    def minus(a, b):
        return [[s - t for s, t in zip(u, v)] for u, v in zip(a, b)]

    @staticmethod
    def times(a, factor):
        return [[factor * s for s in u] for u in a]

    def heun(self, states, change):
        start = change(*states)
        first = [self.minus(s, self.times(c, 0.5 * TIME_STEP)) for s, c in zip(states, start)]
        following = change(*first)
        return [
            self.minus(s, self.times(self.plus(c, d), 0.25 * TIME_STEP)) for s, c, d in zip(states, start, following)
        ]

    def wide_fine(self, pair):
        columns = range(-2, 3)
        parts = [
            [[self.derive(*(self.turned(field[k], c) for field in state)) for c in columns] for state in pair]
            for k in range(len(pair[0][0]))
        ]
        out = [[[], [], []], [[], [], []]]
        for even, odd in parts:
            changes = [self.pair_change(even[i - 1 : i + 2], odd[i - 1 : i + 2]) for i in (1, 2, 3)]
            first = [
                [
                    self.derive(*(column[i] - (0.5 * TIME_STEP) * change[p][i] for i in range(3)))
                    for column, change in zip(columns_of[1:4], changes)
                ]
                for p, columns_of in enumerate((even, odd))
            ]
            following = self.pair_change(*first)
            for p, column in enumerate((even[2], odd[2])):
                for i in range(3):
                    out[p][i].append(column[i] - (0.25 * TIME_STEP) * (changes[1][p][i] + following[p][i]))
        return out

    def turned(self, tile, column):
        return pltpu.roll(tile, -column % self.lanes, 1) if column else tile

    def pair_change(self, even, odd):
        a, b = even[1], odd[1]
        inner = self.cross(a, b)
        upper = self.upper_faces(b, self.raise_up(a))
        lower = self.lower_faces(a, upper)
        out = []
        for (w, m, e), low, high in ((even, lower, inner), (odd, inner, upper)):
            along = zip(self.faces_along(m, e), self.faces_along(w, m))
            out.append([(x - y) + (hi - lo) for (x, y), lo, hi in zip(along, low, high)])
        return out

    def coarse(self, state):
        return self.heun([state], lambda one: [self.coarse_change(one)])[0]

    def fine(self, pair):
        latency = self.fine_fast == "all"
        for _ in range(SUB):
            if self.fine_fast == "wide":
                pair = self.wide_fine(pair)
                continue
            pair = self.heun(pair, lambda even, odd: self.fine_change(even, odd, latency))
        return pair

    def restrict(self, pair):
        return self.times(self.plus(pair[0], pair[1]), 0.5)


class Parareal:
    def __init__(self, scheme, initial):
        self.scheme = scheme
        self.initial = initial
        self.known = {}

    def memo(self, key, build):
        if key not in self.known:
            self.known[key] = build()
        return self.known[key]

    def coarse_state(self, sweep, n):
        sweep = min(sweep, n)

        def build():
            s = self.scheme
            if n == 0:
                return s.restrict(self.initial)
            stepped = self.coarse_step(sweep, n - 1)
            if sweep == 0:
                return stepped
            correction = s.minus(s.restrict(self.fine_run(sweep, n - 1)), self.coarse_step(sweep - 1, n - 1))
            return s.plus(stepped, correction)

        return self.memo(("c", sweep, n), build)

    def coarse_step(self, sweep, n):
        sweep = min(sweep, n)
        return self.memo(("k", sweep, n), lambda: self.scheme.coarse(self.coarse_state(sweep, n)))

    def fine_run(self, sweep, n):
        sweep = 1 if n == 0 else sweep

        def build():
            if n == 0:
                start = self.initial
            elif sweep == 1:
                state = self.coarse_state(0, n)
                start = [state, state]
            else:
                start = self.end(sweep - 1, n - 1)
            return self.scheme.fine(start)

        return self.memo(("f", sweep, n), build)

    def end(self, sweep, n):
        def build():
            s = self.scheme
            refined = self.fine_run(sweep, n)
            renewed, previous = self.coarse_step(sweep, n), self.coarse_step(sweep - 1, n)
            return [s.minus(s.plus(renewed, part), previous) for part in refined]

        return self.memo(("e", sweep, n), build)


def run_of(live_ref, near_ref, blocks):
    slot = jnp.int32(0)
    count = jnp.int32(0)
    for k in range(blocks):
        slot = jnp.where((live_ref[k] == 1) & (near_ref[0, k] == blocks), k, slot)
        count += live_ref[k]
    slots = [slot]
    for _ in range(blocks - 1):
        following = near_ref[1, slots[-1]]
        slots.append(jnp.where(following < blocks, following, slots[-1]))
    return slots, count


def load_fields(depth_ref, momentum_ref, slot):
    rows = depth_ref.shape[1] // 2
    return [
        ref[pl.ds(parity, rows, stride=2), :]
        for parity in range(2)
        for ref in (depth_ref.at[slot], momentum_ref.at[slot, 0], momentum_ref.at[slot, 1])
    ]


def pack(pieces, start, rim):
    rows, lanes = pieces[0].shape
    lane = lane_of((rows, lanes))
    per_tile = lanes // rim
    tiles = []
    for i, piece in enumerate(pieces):
        place = (i % per_tile) * rim
        moved = pltpu.roll(piece, (place - start) % lanes, 1)
        if place == 0:
            tiles.append(moved)
        else:
            tiles[-1] = jnp.where(lane >= place, moved, tiles[-1])
    return tiles


def unpack(packed_ref, index, place, rim):
    lanes = packed_ref.shape[2]
    per_tile = lanes // rim
    source = (index % per_tile) * rim
    return pltpu.roll(packed_ref[index // per_tile], (place - source) % lanes, 1)


def send_kernel(
    rim, slices, depth_hbm, momentum_hbm, live_hbm, near_hbm, east_ref, west_ref, run_ref, edge_ref, place_ref,
    depth_ref, momentum_ref, live_ref, near_ref, sems,
):
    copies = [
        pltpu.make_async_copy(source, target, sems.at[i])
        for i, (source, target) in enumerate(
            ((live_hbm, live_ref), (near_hbm, near_ref), (depth_hbm, depth_ref), (momentum_hbm, momentum_ref))
        )
    ]
    for copy in copies:
        copy.start()
    own, owner = lax.axis_index("tm"), lax.axis_index("space")
    for copy in copies:
        copy.wait()
    blocks, height, lanes = depth_ref.shape
    rows = height // 2
    slots, count = run_of(live_ref, near_ref, blocks)
    tiles = [load_fields(depth_ref, momentum_ref, slot) for slot in slots]
    first, last = tiles[0], tiles[-1]
    for i, tile in enumerate(pack(last, lanes - rim, rim)):
        east_ref[i] = tile
    for i, tile in enumerate(pack(first, 0, rim)):
        west_ref[i] = tile
    for k, fields in enumerate(tiles):
        for i in range(6):
            run_ref[k, i] = fields[i]
        place_ref[k] = jnp.full((rows, lanes), jnp.where(k < count, slots[k], -1), jnp.int32)
    early = (owner == 0) & (own > 0) & (slices <= SPLIT_SLICES)
    length = jnp.where(own < SHORT_SLICES, blocks, count)
    case = (own * blocks + length - 1) + jnp.where(early, slices * blocks, 0)
    place_ref[blocks] = jnp.full((rows, lanes), case, jnp.int32)
    place_ref[blocks + 1] = jnp.full((rows, lanes), own, jnp.int32)
    lane = lane_of((rows, lanes))
    for i, (head, tail) in enumerate(zip(first, last)):
        if edge_ref.shape[0] == 1:
            edge_ref[0, i] = jnp.where(lane < 2 * rim, head, pltpu.roll(tail, 4 * rim, 1))
        else:
            edge_ref[0, i] = head
            edge_ref[1, i] = pltpu.roll(tail, lanes // 2, 1)


def as_initial(tiles):
    return [[[tile[3 * parity + i] for tile in tiles] for i in range(3)] for parity in range(2)]


def interior_graph(run_ref, length, n):
    blocks, _, rows, lanes = run_ref.shape
    tiles = [[run_ref[k, i] for i in range(6)] for k in range(length)]
    fast = length < blocks or n < SHORT_SLICES
    return Parareal(Scheme((rows, lanes), True, "all" if fast else "", True), as_initial(tiles))


def store_end(graph, n, length, out_ref):
    ending = graph.end(KITER, n)
    for k in range(length):
        for i in range(6):
            out_ref[k, i] = ending[i // 3][i % 3][k]


def lengths(n, blocks):
    return [blocks] if n < SHORT_SLICES else range(blocks, 0, -1)


def early_part(n, length, blocks):
    keys = [key for m in range(n) for key in (("k", 0, m), ("f", 1, m))]
    return keys + [("k", 1, 1), ("f", 2, 1)] if n > 2 and length == blocks else keys


def early_kernel(slices, run_ref, place_ref, west_ref, west_out_ref, kept_ref):
    blocks = run_ref.shape[0]
    case = place_ref[blocks][0, 0]

    def work(n, length):
        graph = interior_graph(run_ref, length, n)
        place = 0
        for kind, sweep, m in early_part(n, length, blocks):
            if kind == "k":
                fields = graph.coarse_step(sweep, m)
            else:
                fields = [field for part in graph.fine_run(sweep, m) for field in part]
            for field in fields:
                for tile in field:
                    kept_ref[place] = tile
                    place += 1

    @pl.when(case >= slices * blocks)
    def _():
        for n in reversed(range(1, slices)):
            for length in lengths(n, blocks):
                pl.when(case == (slices + n) * blocks + length - 1)(functools.partial(work, n, length))


def late_kernel(slices, run_ref, place_ref, *refs):
    out_ref = refs[-1]
    blocks = run_ref.shape[0]

    def whole(n, length):
        store_end(interior_graph(run_ref, length, n), n, length, out_ref)

    def rest(n, length):
        graph = interior_graph(run_ref, length, n)
        place = 0
        for kind, sweep, m in early_part(n, length, blocks):
            fields = []
            for _ in range(3 if kind == "k" else 6):
                fields.append([refs[0][place + k] for k in range(length)])
                place += length
            graph.known[kind, sweep, m] = fields if kind == "k" else [fields[:3], fields[3:]]
        store_end(graph, n, length, out_ref)

    if len(refs) == 1:
        own = place_ref[blocks + 1][0, 0]
        for n in range(slices):
            pl.when(own == n)(functools.partial(whole, n, blocks))
        return
    case = place_ref[blocks][0, 0]
    for n in reversed(range(slices)):
        for length in lengths(n, blocks):
            pl.when(case == n * blocks + length - 1)(functools.partial(whole, n, length))
            if n > 0:
                pl.when(case == (slices + n) * blocks + length - 1)(functools.partial(rest, n, length))


def edge_kernel(rim, slices, inner_ref, edge_ref, west_ref, east_ref, place_ref, out_ref):
    blocks, _, rows, lanes = inner_ref.shape
    edges = edge_ref.shape[0]
    own = place_ref[blocks + 1][0, 0]
    for n in reversed(range(slices)):

        @pl.when(own == n)
        def _(n=n):
            lane = lane_of((rows, lanes))
            tiles = [[] for _ in range(edges)]
            for i in range(6):
                west = unpack(west_ref, i, lanes - rim, rim)
                east_start = 4 * rim if edges == 1 else lanes // 2
                east = unpack(east_ref, i, east_start, rim)
                tiles[-1].append(jnp.where(lane < east_start, edge_ref[edges - 1, i], east))
                tiles[0][i:] = [jnp.where(lane < lanes - rim, tiles[0][i] if edges == 1 else edge_ref[0, i], west)]
            ending = Parareal(Scheme((rows, lanes), False, "wide" if n < 2 else "all", True), as_initial(tiles)).end(KITER, n)
            places = [place_ref[k] for k in range(blocks)]
            lasts = [
                (places[k] >= 0) & (places[k + 1] < 0) if k + 1 < blocks else places[k] >= 0 for k in range(blocks)
            ]
            for i in range(6):
                result = ending[i // 3][i % 3]
                tail = pltpu.roll(result[-1], (-4 * rim if edges == 1 else lanes // 2) % lanes, 1)
                merged = []
                for k in range(blocks):
                    tile = jnp.where(lasts[k] & (lane >= lanes - rim), tail, inner_ref[k, i])
                    merged.append(jnp.where(lane < rim, result[0], tile) if k == 0 else tile)
                for slot in range(blocks):
                    chosen = jnp.zeros((rows, lanes), jnp.float32)
                    for k in range(blocks):
                        chosen = jnp.where(places[k] == slot, merged[k], chosen)
                    out_ref[slot, i % 3, pl.ds(i // 3, rows, stride=2), :] = chosen


def local(water_depth, momentum, slot_live, neighbours):
    blocks, height, lanes = water_depth.shape
    rows = height // 2
    slices = lax.axis_size("tm")
    owners = lax.axis_size("space")
    rim = 2 * (slices - 1) + 2 * SUB * KITER - 2
    strip = jax.ShapeDtypeStruct((-(-6 // (lanes // rim)), rows, lanes), jnp.float32)
    edge = jax.ShapeDtypeStruct((1 if 6 * rim <= lanes else 2, 6, rows, lanes), jnp.float32)
    run = jax.ShapeDtypeStruct((blocks, 6, rows, lanes), jnp.float32)
    place = jax.ShapeDtypeStruct((blocks + 2, rows, lanes), jnp.int32)
    whole = jax.ShapeDtypeStruct((blocks, 3, height, lanes), jnp.float32)
    vmem = pl.BlockSpec(memory_space=pltpu.VMEM)
    hbm = pl.BlockSpec(memory_space=pltpu.HBM)
    across = [tm ^ 1 if tm < 2 <= slices else tm for tm in range(slices)]
    up = [(tm * owners + i, across[tm] * owners + (i + 1) % owners) for tm in range(slices) for i in range(owners)]
    down = [(across[j // owners] * owners + j % owners, across[i // owners] * owners + i % owners) for i, j in up]

    params = pltpu.CompilerParams(vmem_limit_bytes=16 * 1024 * 1024)
    east_rim, west_rim, tiles, edges, places = pl.pallas_call(
        functools.partial(send_kernel, rim, slices),
        out_shape=(strip, strip, run, edge, place),
        in_specs=[hbm] * 4,
        out_specs=(vmem,) * 5,
        scratch_shapes=[
            pltpu.VMEM(water_depth.shape, jnp.float32),
            pltpu.VMEM(momentum.shape, jnp.float32),
            pltpu.SMEM(slot_live.shape, jnp.int32),
            pltpu.SMEM(neighbours.shape[::-1], jnp.int32),
            pltpu.SemaphoreType.DMA((4,)),
        ],
        compiler_params=params,
        name="send",
    )(*(pltpu.with_memory_space_constraint(x, pltpu.HBM) for x in (water_depth, momentum, slot_live, neighbours.T)))
    from_west = lax.ppermute(east_rim, ("tm", "space"), up)
    cost = pl.CostEstimate(flops=10_000_000, bytes_accessed=200_000, transcendentals=0)
    kept = ()
    if slices <= SPLIT_SLICES:
        west_rim, *kept = pl.pallas_call(
            functools.partial(early_kernel, slices),
            out_shape=(strip, jax.ShapeDtypeStruct((9 * blocks * slices, rows, lanes), jnp.float32)),
            in_specs=[vmem] * 3,
            out_specs=(vmem, vmem),
            input_output_aliases={2: 0},
            compiler_params=params,
            cost_estimate=cost,
            name="interior_early",
        )(tiles, places, west_rim)
    from_east = lax.ppermute(west_rim, ("tm", "space"), down)
    inner = pl.pallas_call(
        functools.partial(late_kernel, slices),
        out_shape=run,
        in_specs=[vmem] * (2 + len(kept)),
        out_specs=vmem,
        compiler_params=params,
        cost_estimate=cost,
        name="interior_late",
    )(tiles, places, *kept)
    ends = pl.pallas_call(
        functools.partial(edge_kernel, rim, slices),
        out_shape=whole,
        in_specs=[vmem] * 5,
        out_specs=vmem,
        compiler_params=params,
        name="edges",
    )(inner, edges, from_west, from_east, places)
    return ends[None]


def solution(mesh):
    placed = (P("space", None, None), P("space", None, None, None), P("space"), P("space", None))
    return jax.shard_map(
        local,
        mesh=mesh,
        in_specs=placed,
        out_specs=P("tm", "space", None, None, None),
        check_vma=False,
    )
```

```python
import functools

import jax
import jax.numpy as jnp
from jax import lax
from jax.experimental import pallas as pl
from jax.experimental.pallas import tpu as pltpu
from jax.sharding import PartitionSpec as P

SUB = 3
KITER = 2
TIME_STEP = 0.15
SHORT_SLICES = 2
SPLIT_SLICES = 4


def lane_of(shape):
    return lax.broadcasted_iota(jnp.int32, shape, 1)


def row_of(shape):
    return lax.broadcasted_iota(jnp.int32, shape, 0)


class Scheme:
    def __init__(self, shape, linked, fine_fast, coarse_fast):
        self.rows, self.lanes = shape
        self.linked = linked
        self.fine_fast = fine_fast
        self.coarse_fast = coarse_fast
        lane, row = lane_of(shape), row_of(shape)
        self.is_first_lane = lane == 0
        self.is_last_lane = lane == self.lanes - 1
        self.is_first_row = row == 0
        self.is_last_row = row == self.rows - 1

    def east(self, tiles):
        rolled = [pltpu.roll(tile, self.lanes - 1, 1) for tile in tiles]
        if not self.linked:
            return rolled
        return [
            jnp.where(self.is_last_lane, rolled[k + 1], rolled[k]) if k + 1 < len(rolled) else rolled[k]
            for k in range(len(rolled))
        ]

    def west(self, tiles):
        rolled = [pltpu.roll(tile, 1, 1) for tile in tiles]
        if not self.linked:
            return rolled
        return [jnp.where(self.is_first_lane, rolled[k - 1], rolled[k]) if k else rolled[k] for k in range(len(rolled))]

    def above(self, tile):
        return pltpu.roll(tile, self.rows - 1, 0)

    def below(self, tile):
        return pltpu.roll(tile, 1, 0)

    @staticmethod
    def derive(h, hu, hv, needed=(3, 4, 5, 6, 7)):
        root = lax.rsqrt(h)
        celerity = h * root
        inverse = root * root
        u = hu * inverse
        p = (0.5 * h) * h
        part = [h, hu, hv, hu * u + p, hv * u, None, jnp.abs(u) + celerity, None]
        if 5 in needed:
            q = hv * inverse
            part[5] = hv * q + p
            part[7] = jnp.abs(q) + celerity
        return part

    def derived(self, state):
        return [self.derive(h, hu, hv) for h, hu, hv in zip(*state)]

    def moved(self, parts, shift):
        states = zip(*(shift([part[i] for part in parts]) for i in (0, 1, 2)))
        return [self.derive(h, hu, hv, ()) for h, hu, hv in states]

    @staticmethod
    def faces_along(lower, upper):
        bound = jnp.maximum(lower[6], upper[6])
        return [(lower[f] + upper[f]) - bound * (upper[v] - lower[v]) for v, f in ((0, 1), (1, 3), (2, 4))]

    def along(self, parts, latency):
        east = [self.faces_along(a, b) for a, b in zip(parts, self.moved(parts, self.east))]
        if not latency:
            west = list(zip(*(self.west([face[i] for face in east]) for i in range(3))))
        else:
            west = [self.faces_along(a, b) for a, b in zip(self.moved(parts, self.west), parts)]
        return [[e[i] - w[i] for e, w in zip(east, west)] for i in range(3)]

    @staticmethod
    def cross(lower, upper):
        bound = jnp.maximum(lower[7], upper[7])
        return [
            (lower[f] + upper[f]) - bound * (upper[v] - lower[v]) for v, f in ((0, 2), (1, 4), (2, 5))
        ]

    def upper_faces(self, top, raised):
        faces = self.cross(top, raised)
        wall = 2.0 * (top[5] + top[7] * top[2])
        return [
            jnp.where(self.is_last_row, 0.0, faces[0]),
            jnp.where(self.is_last_row, 0.0, faces[1]),
            jnp.where(self.is_last_row, wall, faces[2]),
        ]

    def lower_faces(self, bottom, faces):
        wall = 2.0 * (bottom[5] - bottom[7] * bottom[2])
        lowered = [self.below(face) for face in faces]
        return [lowered[0], lowered[1], jnp.where(self.is_first_row, wall, lowered[2])]

    def raise_up(self, part):
        return [self.above(part[i]) if i in (0, 1, 2, 4, 5, 7) else None for i in range(8)]

    def fine_change(self, even, odd, latency):
        even_parts, odd_parts = self.derived(even), self.derived(odd)
        even_x, odd_x = self.along(even_parts, latency), self.along(odd_parts, latency)
        even_out, odd_out = [[], [], []], [[], [], []]
        for k, (a, b) in enumerate(zip(even_parts, odd_parts)):
            inner = self.cross(a, b)
            upper = self.upper_faces(b, self.raise_up(a))
            lower = self.lower_faces(a, upper)
            for i in range(3):
                even_out[i].append(even_x[i][k] + (inner[i] - lower[i]))
                odd_out[i].append(odd_x[i][k] + (upper[i] - inner[i]))
        return even_out, odd_out

    def coarse_change(self, state):
        parts = self.derived(state)
        x = self.along(parts, self.coarse_fast)
        out = [[], [], []]
        for k, a in enumerate(parts):
            upper = self.upper_faces(a, self.raise_up(a))
            lower = self.lower_faces(a, upper)
            for i in range(3):
                out[i].append(SUB * x[i][k] + (upper[i] - lower[i]))
        return out

    @staticmethod
    def plus(a, b):
        return [[s + t for s, t in zip(u, v)] for u, v in zip(a, b)]

    @staticmethod
    def minus(a, b):
        return [[s - t for s, t in zip(u, v)] for u, v in zip(a, b)]

    @staticmethod
    def times(a, factor):
        return [[factor * s for s in u] for u in a]

    def heun(self, states, change):
        start = change(*states)
        first = [self.minus(s, self.times(c, 0.5 * TIME_STEP)) for s, c in zip(states, start)]
        following = change(*first)
        return [
            self.minus(s, self.times(self.plus(c, d), 0.25 * TIME_STEP)) for s, c, d in zip(states, start, following)
        ]

    def wide_fine(self, pair):
        columns = range(-2, 3)
        parts = [
            [[self.derive(*(self.turned(field[k], c) for field in state)) for c in columns] for state in pair]
            for k in range(len(pair[0][0]))
        ]
        out = [[[], [], []], [[], [], []]]
        for even, odd in parts:
            changes = [self.pair_change(even[i - 1 : i + 2], odd[i - 1 : i + 2]) for i in (1, 2, 3)]
            first = [
                [
                    self.derive(*(column[i] - (0.5 * TIME_STEP) * change[p][i] for i in range(3)))
                    for column, change in zip(columns_of[1:4], changes)
                ]
                for p, columns_of in enumerate((even, odd))
            ]
            following = self.pair_change(*first)
            for p, column in enumerate((even[2], odd[2])):
                for i in range(3):
                    out[p][i].append(column[i] - (0.25 * TIME_STEP) * (changes[1][p][i] + following[p][i]))
        return out

    def turned(self, tile, column):
        return pltpu.roll(tile, -column % self.lanes, 1) if column else tile

    def pair_change(self, even, odd):
        a, b = even[1], odd[1]
        inner = self.cross(a, b)
        upper = self.upper_faces(b, self.raise_up(a))
        lower = self.lower_faces(a, upper)
        out = []
        for (w, m, e), low, high in ((even, lower, inner), (odd, inner, upper)):
            along = zip(self.faces_along(m, e), self.faces_along(w, m))
            out.append([(x - y) + (hi - lo) for (x, y), lo, hi in zip(along, low, high)])
        return out

    def coarse(self, state):
        return self.heun([state], lambda one: [self.coarse_change(one)])[0]

    def fine(self, pair):
        latency = self.fine_fast == "all"
        for _ in range(SUB):
            if self.fine_fast == "wide":
                pair = self.wide_fine(pair)
                continue
            pair = self.heun(pair, lambda even, odd: self.fine_change(even, odd, latency))
        return pair

    def restrict(self, pair):
        return self.times(self.plus(pair[0], pair[1]), 0.5)


class Parareal:
    def __init__(self, scheme, initial):
        self.scheme = scheme
        self.initial = initial
        self.known = {}

    def memo(self, key, build):
        if key not in self.known:
            self.known[key] = build()
        return self.known[key]

    def coarse_state(self, sweep, n):
        sweep = min(sweep, n)

        def build():
            s = self.scheme
            if n == 0:
                return s.restrict(self.initial)
            stepped = self.coarse_step(sweep, n - 1)
            if sweep == 0:
                return stepped
            correction = s.minus(s.restrict(self.fine_run(sweep, n - 1)), self.coarse_step(sweep - 1, n - 1))
            return s.plus(stepped, correction)

        return self.memo(("c", sweep, n), build)

    def coarse_step(self, sweep, n):
        sweep = min(sweep, n)
        return self.memo(("k", sweep, n), lambda: self.scheme.coarse(self.coarse_state(sweep, n)))

    def fine_run(self, sweep, n):
        sweep = 1 if n == 0 else sweep

        def build():
            if n == 0:
                start = self.initial
            elif sweep == 1:
                state = self.coarse_state(0, n)
                start = [state, state]
            else:
                start = self.end(sweep - 1, n - 1)
            return self.scheme.fine(start)

        return self.memo(("f", sweep, n), build)

    def end(self, sweep, n):
        def build():
            s = self.scheme
            refined = self.fine_run(sweep, n)
            renewed, previous = self.coarse_step(sweep, n), self.coarse_step(sweep - 1, n)
            return [s.minus(s.plus(renewed, part), previous) for part in refined]

        return self.memo(("e", sweep, n), build)


def run_of(live_ref, near_ref, blocks):
    slot = jnp.int32(0)
    count = jnp.int32(0)
    for k in range(blocks):
        slot = jnp.where((live_ref[k] == 1) & (near_ref[0, k] == blocks), k, slot)
        count += live_ref[k]
    slots = [slot]
    for _ in range(blocks - 1):
        following = near_ref[1, slots[-1]]
        slots.append(jnp.where(following < blocks, following, slots[-1]))
    return slots, count


def load_fields(depth_ref, momentum_ref, slot):
    rows = depth_ref.shape[1] // 2
    return [
        ref[pl.ds(parity, rows, stride=2), :]
        for parity in range(2)
        for ref in (depth_ref.at[slot], momentum_ref.at[slot, 0], momentum_ref.at[slot, 1])
    ]


def pack(pieces, start, rim):
    rows, lanes = pieces[0].shape
    lane = lane_of((rows, lanes))
    per_tile = lanes // rim
    tiles = []
    for i, piece in enumerate(pieces):
        place = (i % per_tile) * rim
        moved = pltpu.roll(piece, (place - start) % lanes, 1)
        if place == 0:
            tiles.append(moved)
        else:
            tiles[-1] = jnp.where(lane >= place, moved, tiles[-1])
    return tiles


def unpack(packed_ref, index, place, rim):
    lanes = packed_ref.shape[2]
    per_tile = lanes // rim
    source = (index % per_tile) * rim
    return pltpu.roll(packed_ref[index // per_tile], (place - source) % lanes, 1)


def send_kernel(
    rim, slices, depth_hbm, momentum_hbm, live_hbm, near_hbm, east_ref, west_ref, run_ref, edge_ref, place_ref,
    depth_ref, momentum_ref, live_ref, near_ref, sems,
):
    copies = [
        pltpu.make_async_copy(source, target, sems.at[i])
        for i, (source, target) in enumerate(
            ((live_hbm, live_ref), (near_hbm, near_ref), (depth_hbm, depth_ref), (momentum_hbm, momentum_ref))
        )
    ]
    for copy in copies:
        copy.start()
    own, owner = lax.axis_index("tm"), lax.axis_index("space")
    blocks, height, lanes = depth_ref.shape
    rows = height // 2
    for copy in copies[:2]:
        copy.wait()
    slots, count = run_of(live_ref, near_ref, blocks)
    for k in range(blocks):
        place_ref[k] = jnp.full((rows, lanes), jnp.where(k < count, slots[k], -1), jnp.int32)
    early = (owner == 0) & (own > 0) & (slices <= SPLIT_SLICES)
    length = jnp.where(own < SHORT_SLICES, blocks, count)
    case = (own * blocks + length - 1) + jnp.where(early, slices * blocks, 0)
    place_ref[blocks] = jnp.full((rows, lanes), case, jnp.int32)
    place_ref[blocks + 1] = jnp.full((rows, lanes), own, jnp.int32)
    for copy in copies[2:]:
        copy.wait()
    last = load_fields(depth_ref, momentum_ref, slots[-1])
    for i, tile in enumerate(pack(last, lanes - rim, rim)):
        east_ref[i] = tile
    tiles = [load_fields(depth_ref, momentum_ref, slot) for slot in slots[:-1]] + [last]
    first = tiles[0]
    for i, tile in enumerate(pack(first, 0, rim)):
        west_ref[i] = tile
    for k, fields in enumerate(tiles):
        for i in range(6):
            run_ref[k, i] = fields[i]
    lane = lane_of((rows, lanes))
    for i, (head, tail) in enumerate(zip(first, last)):
        if edge_ref.shape[0] == 1:
            edge_ref[0, i] = jnp.where(lane < 2 * rim, head, pltpu.roll(tail, 4 * rim, 1))
        else:
            edge_ref[0, i] = head
            edge_ref[1, i] = pltpu.roll(tail, lanes // 2, 1)


def as_initial(tiles):
    return [[[tile[3 * parity + i] for tile in tiles] for i in range(3)] for parity in range(2)]


def interior_graph(run_ref, length, n, part=False):
    blocks, _, rows, lanes = run_ref.shape
    tiles = [[run_ref[k, i] for i in range(6)] for k in range(length)]
    fast = part or length < blocks or n < SHORT_SLICES
    return Parareal(Scheme((rows, lanes), True, "all" if fast else "", True), as_initial(tiles))


def store_end(graph, n, length, out_ref):
    ending = graph.end(KITER, n)
    for k in range(length):
        for i in range(6):
            out_ref[k, i] = ending[i // 3][i % 3][k]


def lengths(n, blocks):
    return [blocks] if n < SHORT_SLICES else range(blocks, 0, -1)


def early_part(n, length, blocks):
    keys = [key for m in range(n) for key in (("k", 0, m), ("f", 1, m))]
    return keys + [("k", 1, 1), ("f", 2, 1)] if n > 2 and length == blocks else keys


def early_kernel(slices, run_ref, place_ref, west_ref, west_out_ref, kept_ref):
    blocks = run_ref.shape[0]
    case = place_ref[blocks][0, 0]

    def work(n, length):
        graph = interior_graph(run_ref, length, n, True)
        place = 0
        for kind, sweep, m in early_part(n, length, blocks):
            if kind == "k":
                fields = graph.coarse_step(sweep, m)
            else:
                fields = [field for part in graph.fine_run(sweep, m) for field in part]
            for field in fields:
                for tile in field:
                    kept_ref[place] = tile
                    place += 1

    @pl.when(case >= slices * blocks)
    def _():
        for n in reversed(range(1, slices)):
            for length in lengths(n, blocks):
                pl.when(case == (slices + n) * blocks + length - 1)(functools.partial(work, n, length))


def late_kernel(slices, run_ref, place_ref, *refs):
    out_ref = refs[-1]
    blocks = run_ref.shape[0]

    def whole(n, length):
        store_end(interior_graph(run_ref, length, n), n, length, out_ref)

    def rest(n, length):
        graph = interior_graph(run_ref, length, n, True)
        place = 0
        for kind, sweep, m in early_part(n, length, blocks):
            fields = []
            for _ in range(3 if kind == "k" else 6):
                fields.append([refs[0][place + k] for k in range(length)])
                place += length
            graph.known[kind, sweep, m] = fields if kind == "k" else [fields[:3], fields[3:]]
        store_end(graph, n, length, out_ref)

    if len(refs) == 1:
        own = place_ref[blocks + 1][0, 0]
        for n in range(slices):
            pl.when(own == n)(functools.partial(whole, n, blocks))
        return
    case = place_ref[blocks][0, 0]
    for n in reversed(range(slices)):
        for length in lengths(n, blocks):
            pl.when(case == n * blocks + length - 1)(functools.partial(whole, n, length))
            if n > 0:
                pl.when(case == (slices + n) * blocks + length - 1)(functools.partial(rest, n, length))


def edge_kernel(rim, slices, inner_ref, edge_ref, west_ref, east_ref, place_ref, out_ref):
    blocks, _, rows, lanes = inner_ref.shape
    edges = edge_ref.shape[0]
    own = place_ref[blocks + 1][0, 0]
    for n in reversed(range(slices)):

        @pl.when(own == n)
        def _(n=n):
            lane = lane_of((rows, lanes))
            tiles = [[] for _ in range(edges)]
            for i in range(6):
                west = unpack(west_ref, i, lanes - rim, rim)
                east_start = 4 * rim if edges == 1 else lanes // 2
                east = unpack(east_ref, i, east_start, rim)
                tiles[-1].append(jnp.where(lane < east_start, edge_ref[edges - 1, i], east))
                tiles[0][i:] = [jnp.where(lane < lanes - rim, tiles[0][i] if edges == 1 else edge_ref[0, i], west)]
            ending = Parareal(Scheme((rows, lanes), False, "wide" if n < 2 else "all", True), as_initial(tiles)).end(KITER, n)
            places = [place_ref[k] for k in range(blocks)]
            lasts = [
                (places[k] >= 0) & (places[k + 1] < 0) if k + 1 < blocks else places[k] >= 0 for k in range(blocks)
            ]
            for i in range(6):
                result = ending[i // 3][i % 3]
                tail = pltpu.roll(result[-1], (-4 * rim if edges == 1 else lanes // 2) % lanes, 1)
                merged = []
                for k in range(blocks):
                    tile = jnp.where(lasts[k] & (lane >= lanes - rim), tail, inner_ref[k, i])
                    merged.append(jnp.where(lane < rim, result[0], tile) if k == 0 else tile)
                for slot in range(blocks):
                    chosen = jnp.zeros((rows, lanes), jnp.float32)
                    for k in range(blocks):
                        chosen = jnp.where(places[k] == slot, merged[k], chosen)
                    out_ref[slot, i % 3, pl.ds(i // 3, rows, stride=2), :] = chosen


def local(water_depth, momentum, slot_live, neighbours):
    blocks, height, lanes = water_depth.shape
    rows = height // 2
    slices = lax.axis_size("tm")
    owners = lax.axis_size("space")
    rim = 2 * (slices - 1) + 2 * SUB * KITER - 2
    strip = jax.ShapeDtypeStruct((-(-6 // (lanes // rim)), rows, lanes), jnp.float32)
    edge = jax.ShapeDtypeStruct((1 if 6 * rim <= lanes else 2, 6, rows, lanes), jnp.float32)
    run = jax.ShapeDtypeStruct((blocks, 6, rows, lanes), jnp.float32)
    place = jax.ShapeDtypeStruct((blocks + 2, rows, lanes), jnp.int32)
    whole = jax.ShapeDtypeStruct((blocks, 3, height, lanes), jnp.float32)
    vmem = pl.BlockSpec(memory_space=pltpu.VMEM)
    hbm = pl.BlockSpec(memory_space=pltpu.HBM)
    across = [tm ^ 1 if tm < 2 <= slices else tm for tm in range(slices)]
    up = [(tm * owners + i, across[tm] * owners + (i + 1) % owners) for tm in range(slices) for i in range(owners)]
    down = [(across[j // owners] * owners + j % owners, across[i // owners] * owners + i % owners) for i, j in up]

    params = pltpu.CompilerParams(vmem_limit_bytes=16 * 1024 * 1024)
    east_rim, west_rim, tiles, edges, places = pl.pallas_call(
        functools.partial(send_kernel, rim, slices),
        out_shape=(strip, strip, run, edge, place),
        in_specs=[hbm] * 4,
        out_specs=(vmem,) * 5,
        scratch_shapes=[
            pltpu.VMEM(water_depth.shape, jnp.float32),
            pltpu.VMEM(momentum.shape, jnp.float32),
            pltpu.SMEM(slot_live.shape, jnp.int32),
            pltpu.SMEM(neighbours.shape[::-1], jnp.int32),
            pltpu.SemaphoreType.DMA((4,)),
        ],
        compiler_params=params,
        name="send",
    )(*(pltpu.with_memory_space_constraint(x, pltpu.HBM) for x in (water_depth, momentum, slot_live, neighbours.T)))
    from_west = lax.ppermute(east_rim, ("tm", "space"), up)
    cost = pl.CostEstimate(flops=10_000_000, bytes_accessed=200_000, transcendentals=0)
    kept = ()
    if slices <= SPLIT_SLICES:
        west_rim, *kept = pl.pallas_call(
            functools.partial(early_kernel, slices),
            out_shape=(strip, jax.ShapeDtypeStruct((9 * blocks * slices, rows, lanes), jnp.float32)),
            in_specs=[vmem] * 3,
            out_specs=(vmem, vmem),
            input_output_aliases={2: 0},
            compiler_params=params,
            cost_estimate=cost,
            name="interior_early",
        )(tiles, places, west_rim)
    from_east = lax.ppermute(west_rim, ("tm", "space"), down)
    inner = pl.pallas_call(
        functools.partial(late_kernel, slices),
        out_shape=run,
        in_specs=[vmem] * (2 + len(kept)),
        out_specs=vmem,
        compiler_params=params,
        cost_estimate=cost,
        name="interior_late",
    )(tiles, places, *kept)
    ends = pl.pallas_call(
        functools.partial(edge_kernel, rim, slices),
        out_shape=whole,
        in_specs=[vmem] * 5,
        out_specs=vmem,
        compiler_params=params,
        name="edges",
    )(inner, edges, from_west, from_east, places)
    return ends[None]


def solution(mesh):
    placed = (P("space", None, None), P("space", None, None, None), P("space"), P("space", None))
    return jax.shard_map(
        local,
        mesh=mesh,
        in_specs=placed,
        out_specs=P("tm", "space", None, None, None),
        check_vma=False,
    )
```
